32 devices in a mesh: grp: 2 (over x), roll: 8 (over z, y), head: 2 (over core).
Axes of the slice: x: 2, y: 2, z: 4, core: 2. Of those that a mesh axis runs over, the one named last changes fastest.
Arguments:
- store: bfloat16 [8, 1024, 576], P('grp', 'roll'), parts along dimension 0, may hold values from -7 to 7
- queries: bfloat16 [2, 128, 12288], P(None, ('grp', 'roll'), 'head'), parts along dimension 1, may hold values from -7.5 to 7.5
- table: bfloat16 [8192, 576], P('roll'), may hold values from -6 to 6
- w_uk: bfloat16 [64, 128, 512], P('head'), may hold values from -0.5 to 0.5
- w_uv: bfloat16 [64, 512, 128], P('head'), may hold values from -1.796875 to 1.796875
- w_out: bfloat16 [8192, 7168], P('head', 'roll'), may hold values from -0.0625 to 0.0625
- counts: int32 [8], P('grp'), parts along dimension 0, may hold values from 4 to 32, as said below
- prompt_rows: int32 [8], P('grp'), parts along dimension 0, may hold values from 0 to 3, each once
- decode_perm: int32 [16], P('grp'), parts along dimension 0, may hold values from 0 to 7, each once
- token_ids: int32 [128, 2], P('grp'), parts along dimension 0, may hold values from 0 to 8191
Outputs:
- layer_out: bfloat16 [128, 2, 7168], P(('grp', 'head'), None, 'roll'), parts along dimension 0
The draws below stay inside these ranges and needn't reach their ends.
There are 2 independent parts, one for each index of `grp`. The reference program is written for one: setup_inputs(seed, part) draws one part's arguments, and reference() takes and returns one part's arrays. A program takes and returns all parts, laid end to end along the dimension named above; an argument that names none is the same for every part. Nothing has to cross between parts.
Inputs may be any that keep to these rules, and one draw needn't show every extreme that they name: The counts sum to 64; every aligned block of 8 consecutive samples covers at most 3 prompts, and some block covers exactly 3.
All inputs are finite; a program needn't handle non-finite values.
Results may differ from the reference program's by a relative error of at most 0.008.
Values may be sent and summed in bfloat16 or wider, within the bound.
A program may use at most 128 MiB of HBM per device.

```python
import math
import jax
import jax.numpy as jnp
import numpy as np
from jax import lax

D = 7168
KV_RANK = 512
ROPE_DIM = 64
NOPE_DIM = 128
V_DIM = 128
HEADS = 64
S_DEV = 8
STEPS = 2
LEN = 1024
SAMPLES = 64
PROMPTS = 4
VOCAB = 8192
LATENT = 576
QK_DIM = 192
N_ROLL = 8


def draw_store(key, part):
    key = jax.random.fold_in(key, 11)
    key_base = jax.random.fold_in(key, 0)
    shape = (PROMPTS, LEN, LATENT)
    values = jnp.clip(jax.random.normal(key_base, shape, jnp.float32), -6.0, 6.0)
    return values.astype(jnp.bfloat16)


def draw_queries(key, part):
    key = jax.random.fold_in(key, 23)
    key_base = jax.random.fold_in(key, 0)
    shape = (STEPS, SAMPLES, HEADS, QK_DIM)
    values = jnp.clip(jax.random.normal(key_base, shape, jnp.float32), -6.0, 6.0)
    return values.reshape(STEPS, SAMPLES, HEADS * QK_DIM).astype(jnp.bfloat16)


def draw_counts(key, part):
    key = jax.random.fold_in(key, 37)
    key_first, key_weights, key_place, key_flip, key_offset = jax.random.split(key, 5)
    offset = jax.random.randint(key_offset, (), 1, 4)
    first = (offset + 8 + 8 * jax.random.randint(key_first, (), 0, 2)).astype(jnp.int32)
    remaining = PROMPTS - 3
    extra_total = SAMPLES - first - 36 - 4 * remaining
    weights = jax.random.randint(key_weights, (remaining,), 50, 101)
    extras = extra_total * weights // jnp.sum(weights)
    shortfall = extra_total - jnp.sum(extras)
    extras = extras + (jnp.arange(remaining) < shortfall).astype(jnp.int32)
    tail = (4 + extras).astype(jnp.int32)
    peak = jnp.array([32], jnp.int32)
    middle_a = jnp.concatenate([peak, tail])
    middle_b = jnp.concatenate([tail[:1], peak, tail[1:]])
    swap_place = jax.random.randint(key_place, (), 0, 2)
    middle = jnp.where(swap_place == 1, middle_b, middle_a)
    full = jnp.concatenate([jnp.stack([first, jnp.array(4, jnp.int32)]), middle]).astype(jnp.int32)
    flip = jax.random.randint(key_flip, (), 0, 2)
    return jnp.where(flip == 1, full[::-1], full).astype(jnp.int32)


def plant(drawn, key, low, high):
    longest = drawn.shape.index(max(drawn.shape))
    spots = []
    for shift in (0, 1):
        where = [jax.random.randint(jax.random.fold_in(key, axis), (), 0, length) for axis, length in enumerate(drawn.shape)]
        where[longest] = (where[longest] + shift) % drawn.shape[longest]
        spots.append(tuple(where))
    return drawn.at[spots[0]].set(low).at[spots[1]].set(high)


def shard_levels(stream_key, dims, pieces, least, top_value):
    gain, own = 1.0, jax.random.fold_in(stream_key, 6)
    for dim, parts in pieces:
        heights = jnp.exp(jax.random.uniform(jax.random.fold_in(own, dim), (parts,), jnp.float32, least / len(pieces), top_value / len(pieces)))
        gain = gain * jnp.repeat(heights, dims[dim] // parts).reshape([-1 if axis == dim else 1 for axis in range(len(dims))])
    return gain


def rank_bounds(count, skew):
    weights = [(1 << 20) // math.isqrt(rank ** skew) + 1 for rank in range(1, count + 1)]
    deviation = 1 + sum(weights) // (1 << 30)
    return np.cumsum(np.array([max(1, weight // deviation) for weight in weights]))


def ranked(key, dims, amount, lean):
    grid = rank_bounds(amount, lean)
    ticket = jax.random.randint(jax.random.fold_in(key, 1), dims, 0, int(grid[amount - 1]))
    standing = jnp.searchsorted(jnp.asarray(grid, jnp.int32), ticket, side="right")
    return jax.random.permutation(jax.random.fold_in(key, 2), amount)[standing].astype(jnp.int32)


def noise(key, shape, scale, limit, cuts=(), kind=jnp.bfloat16):
    result = jax.random.normal(key, shape, jnp.float32) * scale
    if len(cuts) > 0:
        result = shard_levels(key, shape, cuts, -0.22, 0.18) * result
    return jnp.clip(result, min=-limit, max=limit).astype(kind)


def setup_inputs(seed: int = 0, part: int = 0) -> dict:
    seeds = jax.random.split(jax.random.key(seed), 11)
    part_splits = jax.random.split(jax.random.fold_in(seeds[10], part), 11)
    store = draw_store(jax.random.fold_in(jax.random.fold_in(seeds[10], part), 71), part)
    queries = draw_queries(jax.random.fold_in(jax.random.fold_in(seeds[10], part), 71), part)
    table = noise(seeds[2], (VOCAB, LATENT), 1.0, 6.0, ((0, 8),))
    w_uk = noise(seeds[3], (HEADS, NOPE_DIM, KV_RANK), NOPE_DIM ** -0.5, 0.5, ((0, 2),))
    w_uv = noise(seeds[4], (HEADS, KV_RANK, V_DIM), 0.3, 1.796875, ((0, 2),))
    w_out = noise(seeds[5], (HEADS * V_DIM, D), (HEADS * V_DIM) ** -0.5, 0.0625, ((0, 2), (1, 8)))
    counts = draw_counts(jax.random.fold_in(jax.random.fold_in(seeds[10], part), 71), part)
    prompt_rows = jax.random.permutation(part_splits[7], PROMPTS).astype(jnp.int32)
    decode_perm = jax.random.permutation(part_splits[8], N_ROLL).astype(jnp.int32)
    token_ids = plant(ranked(part_splits[9], (SAMPLES, STEPS), VOCAB, 2), jax.random.fold_in(part_splits[9], 3), 0, VOCAB - 1).astype(jnp.int32)
    return {"store": store, "queries": queries, "table": table, "w_uk": w_uk, "w_uv": w_uv, "w_out": w_out, "counts": counts, "prompt_rows": prompt_rows, "decode_perm": decode_perm, "token_ids": token_ids}


masked_fill = -1e30
rope_base = 10000.0


def rotate_rope(latent_rows, positions):
    half_dim = ROPE_DIM // 2
    freqs = rope_base ** (-jnp.arange(half_dim, dtype=jnp.float32) / half_dim)
    angles = positions[:, None] * freqs[None, :]
    cosine = jnp.cos(angles)
    sine = jnp.sin(angles)
    front = latent_rows[..., KV_RANK:KV_RANK + half_dim]
    behind = latent_rows[..., KV_RANK + half_dim:]
    return jnp.concatenate([latent_rows[..., :KV_RANK], front * cosine - behind * sine, front * sine + behind * cosine], axis=-1)


def reference(store, queries, table, w_uk, w_uv, w_out, counts, prompt_rows, decode_perm, token_ids):
    bound_ends = jnp.cumsum(counts).astype(jnp.int32)
    sample_ids = jnp.arange(SAMPLES, dtype=jnp.int32)
    prompt_of = jnp.sum((bound_ends[None, :] <= sample_ids[:, None]).astype(jnp.int32), axis=1).astype(jnp.int32)
    devices = jnp.arange(N_ROLL, dtype=jnp.int32)
    block_of = jnp.sum(jnp.where(decode_perm[None, :] == devices[:, None], devices[None, :], 0), axis=1).astype(jnp.int32)
    slot_sample = (block_of[:, None] * S_DEV + jnp.arange(S_DEV, dtype=jnp.int32)[None, :]).reshape(-1)
    slot_rows = prompt_rows[prompt_of[slot_sample]].astype(jnp.int32)
    positions = (LEN + jnp.arange(STEPS)).astype(jnp.float32)
    new_latents = rotate_rope(table[token_ids].astype(jnp.float32), positions).astype(jnp.bfloat16)
    query_parts = queries.reshape(STEPS, SAMPLES, HEADS, QK_DIM).transpose(1, 0, 2, 3)
    q_latent = jnp.einsum('sthd,hdc->sthc', query_parts[..., :NOPE_DIM].astype(jnp.float32), w_uk.astype(jnp.float32)).astype(jnp.bfloat16)
    q_full = jnp.concatenate([q_latent, query_parts[..., NOPE_DIM:]], axis=-1)
    w_uv_wide = w_uv.astype(jnp.float32)
    score_scale = QK_DIM ** -0.5
    allowed = jnp.arange(STEPS)[None, :] <= jnp.arange(STEPS)[:, None]

    def one_slot(packed):
        cache_row, q_slot, new_slot = packed
        cache_rows = lax.dynamic_index_in_dim(store, cache_row, 0, keepdims=False).astype(jnp.float32)
        q_wide = q_slot.astype(jnp.float32)
        new_keys = new_slot.astype(jnp.float32)
        cache_scores = jnp.einsum('thc,jc->thj', q_wide, cache_rows) * score_scale
        new_scores = jnp.einsum('thc,uc->thu', q_wide, new_keys) * score_scale
        new_scores = jnp.where(allowed[:, None, :], new_scores, masked_fill)
        row_max = jnp.maximum(jnp.max(cache_scores, axis=-1), jnp.max(new_scores, axis=-1))[..., None]
        cache_exp = jnp.exp(cache_scores - row_max)
        new_exp = jnp.exp(new_scores - row_max)
        denom = jnp.sum(cache_exp, axis=-1, keepdims=True) + jnp.sum(new_exp, axis=-1, keepdims=True)
        cache_probs = (cache_exp / denom).astype(jnp.bfloat16).astype(jnp.float32)
        new_probs = (new_exp / denom).astype(jnp.bfloat16).astype(jnp.float32)
        attended = jnp.einsum('thj,jc->thc', cache_probs, cache_rows[:, :KV_RANK])
        attended = attended + jnp.einsum('thu,uc->thc', new_probs, new_keys[:, :KV_RANK])
        attended = attended.astype(jnp.bfloat16).astype(jnp.float32)
        return jnp.einsum('thc,hcv->thv', attended, w_uv_wide).astype(jnp.bfloat16)

    head_out = lax.map(one_slot, (slot_rows, q_full, new_latents))
    merged = head_out.reshape(SAMPLES * STEPS, HEADS * V_DIM)
    return jnp.dot(merged, w_out, preferred_element_type=jnp.float32).astype(jnp.bfloat16).reshape(SAMPLES, STEPS, D)
```

```python
import functools

import jax
import jax.numpy as jnp
import numpy as np
from jax import lax
from jax.experimental import pallas as pl
from jax.experimental.pallas import tpu as pltpu
from jax.sharding import PartitionSpec as P

KV_RANK = 512
ROPE_DIM = 64
NOPE_DIM = 128


masked_fill = -1e30
rope_base = 10000.0


def pick_values(values, positions):
    matches = positions[..., None] == jnp.arange(values.shape[0], dtype=jnp.int32)
    return jnp.sum(jnp.where(matches, values, 0), axis=-1)


def rotate_rope(latent_rows, positions):
    half_dim = ROPE_DIM // 2
    freqs = rope_base ** (-jnp.arange(half_dim, dtype=jnp.float32) / half_dim)
    angles = positions[:, None] * freqs[None, :]
    cosine = jnp.cos(angles)
    sine = jnp.sin(angles)
    front = latent_rows[..., KV_RANK : KV_RANK + half_dim]
    behind = latent_rows[..., KV_RANK + half_dim :]
    return jnp.concatenate(
        [
            latent_rows[..., :KV_RANK],
            front * cosine - behind * sine,
            front * sine + behind * cosine,
        ],
        axis=-1,
    )


def shards(store, queries, table, w_uk, w_uv, w_out, counts, prompt_rows, decode_perm, token_ids):
    roll_count = lax.axis_size("roll")
    roll_index = lax.axis_index("roll")
    step_count = queries.shape[0]
    slots_dev = queries.shape[1]
    latent_width = store.shape[2]
    cache_len = store.shape[1] * roll_count
    bound_ends = jnp.cumsum(counts)
    sample_ids = jnp.arange(roll_count * slots_dev, dtype=jnp.int32)
    prompt_of = jnp.sum((bound_ends[None, :] <= sample_ids[:, None]).astype(jnp.int32), axis=1)
    devices = jnp.arange(roll_count, dtype=jnp.int32)
    block_of = jnp.sum(
        jnp.where(decode_perm[None, :] == devices[:, None], devices[None, :], 0), axis=1
    )
    slot_offsets = jnp.arange(slots_dev, dtype=jnp.int32)
    slot_prompt = pick_values(prompt_of, block_of[:, None] * slots_dev + slot_offsets[None, :])
    send_rows = pick_values(prompt_rows, slot_prompt).reshape(-1)
    outgoing = jnp.take(store, send_rows, axis=0).reshape(
        roll_count, slots_dev, store.shape[1], latent_width
    )
    incoming = lax.all_to_all(outgoing, "roll", split_axis=0, concat_axis=2, tiled=True)
    cache_rows = incoming.reshape(slots_dev, cache_len, latent_width)
    flat_ids = token_ids.reshape(-1)
    vocab_dev = table.shape[0]
    vocab_base = roll_index * vocab_dev
    one_hot = (
        flat_ids[:, None] - vocab_base == jnp.arange(vocab_dev, dtype=jnp.int32)[None, :]
    ).astype(jnp.bfloat16)
    looked = lax.psum_scatter(
        jnp.dot(one_hot, table, preferred_element_type=jnp.float32),
        "roll",
        scatter_dimension=0,
        tiled=True,
    )
    looked = (
        looked.astype(jnp.bfloat16).astype(jnp.float32).reshape(slots_dev, step_count, latent_width)
    )
    positions = (cache_len + jnp.arange(step_count)).astype(jnp.float32)
    new_latents = rotate_rope(looked, positions).astype(jnp.bfloat16)
    head_count = w_uk.shape[0]
    query_parts = queries.reshape(step_count, slots_dev, head_count, -1)
    q_latent = jnp.einsum(
        "tshd,hdc->tshc", query_parts[..., :NOPE_DIM], w_uk, preferred_element_type=jnp.float32
    ).astype(jnp.bfloat16)
    q_full = jnp.concatenate([q_latent, query_parts[..., NOPE_DIM:]], axis=-1)
    score_scale = (NOPE_DIM + ROPE_DIM) ** (-0.5)
    cache_scores = (
        jnp.einsum("tshc,sjc->tshj", q_full, cache_rows, preferred_element_type=jnp.float32)
        * score_scale
    )
    new_scores = (
        jnp.einsum("tshc,suc->tshu", q_full, new_latents, preferred_element_type=jnp.float32)
        * score_scale
    )
    allowed = jnp.arange(step_count)[None, :] <= jnp.arange(step_count)[:, None]
    new_scores = jnp.where(allowed[:, None, None, :], new_scores, masked_fill)
    row_max = jnp.maximum(jnp.max(cache_scores, axis=-1), jnp.max(new_scores, axis=-1))[..., None]
    cache_exp = jnp.exp(cache_scores - row_max)
    new_exp = jnp.exp(new_scores - row_max)
    denom = jnp.sum(cache_exp, axis=-1, keepdims=True) + jnp.sum(new_exp, axis=-1, keepdims=True)
    cache_probs = (cache_exp / denom).astype(jnp.bfloat16)
    new_probs = (new_exp / denom).astype(jnp.bfloat16)
    attended = jnp.einsum(
        "tshj,sjc->tshc", cache_probs, cache_rows[..., :KV_RANK], preferred_element_type=jnp.float32
    )
    attended = attended + jnp.einsum(
        "tshu,suc->tshc", new_probs, new_latents[..., :KV_RANK], preferred_element_type=jnp.float32
    )
    attended = attended.astype(jnp.bfloat16)
    head_out = jnp.einsum(
        "tshc,hcv->tshv", attended, w_uv, preferred_element_type=jnp.float32
    ).astype(jnp.bfloat16)
    slot_major = head_out.transpose(1, 0, 2, 3).reshape(slots_dev * step_count, -1)
    partial_out = jnp.dot(
        lax.all_gather(slot_major, "roll", axis=0, tiled=True),
        w_out,
        preferred_element_type=jnp.float32,
    )
    summed = lax.psum_scatter(partial_out, "head", scatter_dimension=0, tiled=True)
    return summed.astype(jnp.bfloat16).reshape(-1, step_count, w_out.shape[1])


def contract_last(a, b):
    return lax.dot_general(a, b, (((1,), (1,)), ((), ())), preferred_element_type=jnp.float32)


def fused_kernel(
    counts, prompt_rows, decode_perm, token_ids, rope_cos, rope_sin, queries, store, table, w_uk, w_uv, w_out,
    out,
    kv, table_v, uk_v, uv_v, wout_v, contrib, tokens, new_keys, q_all, row_of, m_ref, l_ref, acc, att, heads_all, part, other,
    load_sem, kv_recv, own_send, z_send, y_send, sib_send, tok_recv, tok_send,
    ho_recv, ho_own_send, ho_z_send, ho_y_send, ex_sem,
):
    me = lax.axis_index("roll")
    core = lax.axis_index("head")
    z, y = me // 2, me % 2
    flip = 1 - y
    prompts = store.shape[0]
    half = prompts // 2
    block = store.shape[1]
    head_count = uk_v.shape[0]
    last = 3

    def to(roll):
        return {"roll": roll}

    sibling = {"head": 1 - core}
    mine = pl.ds(half * core, half)

    def remote(src, dst, send, recv, device):
        return pltpu.make_async_remote_copy(
            src_ref=src, dst_ref=dst, send_sem=send, recv_sem=recv, device_id=device,
            device_id_type=pl.DeviceIdType.MESH,
        )

    loads = [
        pltpu.make_async_copy(table, table_v, load_sem.at[0]),
        pltpu.make_async_copy(w_uk, uk_v, load_sem.at[1]),
        pltpu.make_async_copy(store, kv.at[me], load_sem.at[2]),
        pltpu.make_async_copy(w_uv, uv_v, load_sem.at[3]),
        pltpu.make_async_copy(w_out, wout_v, load_sem.at[4]),
    ]
    for load in loads:
        load.start()

    barrier = pltpu.get_barrier_semaphore()
    for k in range(1, 8):
        pl.semaphore_signal(barrier, inc=1, device_id=to((me + k) % 8), device_id_type=pl.DeviceIdType.MESH)
    pl.semaphore_signal(barrier, inc=1, device_id=sibling, device_id_type=pl.DeviceIdType.MESH)
    pl.semaphore_wait(barrier, 8)

    near = jnp.minimum(z, last - z)

    def layer(i):
        up = jnp.where(i == 0, near, jnp.where(i > near, i, i - 1))
        return jnp.where(z <= 1, up, last - up)

    own_block = store.at[mine]

    def own_copy(step):
        slot = 0 if step < 0 else 1
        return remote(own_block, kv.at[me, mine], own_send.at[slot], kv_recv.at[me, core], to(me + 2 * step))

    def z_copy(i):
        src = layer(i) * 2 + y
        step = jnp.where(layer(i) < z, 2, -2)
        return remote(kv.at[src, mine], kv.at[src, mine], z_send.at[i], kv_recv.at[src, core], to(me + step))

    def z_goes_on(i):
        return jnp.where(layer(i) < z, z < last, z > 0)

    def y_copy(i):
        src = layer(i) * 2 + y
        return remote(kv.at[src, mine], kv.at[src, mine], y_send.at[i], kv_recv.at[src, core], to(z * 2 + flip))

    def own_y_copy():
        return remote(own_block, kv.at[me, mine], y_send.at[0], kv_recv.at[me, core], to(z * 2 + flip))

    def sib_copy(i, side):
        src = layer(i) * 2 + side
        return remote(kv.at[src, mine], kv.at[src, mine], sib_send.at[i, side], kv_recv.at[src, core], sibling)

    def await_block(src, which):
        ref = kv.at[src, pl.ds(half * which, half)]
        pltpu.make_async_copy(ref, ref, kv_recv.at[src, which]).wait()

    own_y_copy().start()

    @pl.when(z < last)
    def _():
        own_copy(1).start()

    @pl.when(z > 0)
    def _():
        own_copy(-1).start()

    loads[0].wait()
    rows_here = table_v.shape[0]
    spots = lax.broadcasted_iota(jnp.int32, (token_ids.shape[0], rows_here), 1) + me * rows_here
    picked = []
    for t in range(2):
        hot = jnp.where(token_ids[:, t : t + 1] == spots, 1.0, 0.0).astype(jnp.bfloat16)
        got = jnp.dot(hot, table_v[...], preferred_element_type=jnp.float32)
        picked.append(got.reshape(8, 8, got.shape[-1]))
    contrib[...] = jnp.concatenate(picked, axis=1).astype(jnp.bfloat16)

    def tok_copy(k):
        dst = (me + k) % 8
        return remote(contrib.at[dst], tokens.at[me], tok_send.at[dst], tok_recv.at[me], to(dst))

    for k in range(1, 8):
        tok_copy(k).start()

    loads[1].wait()

    def head_pair(p, carry):
        cols = pl.ds(pl.multiple_of(p * 384, 128), 384)
        both = jnp.concatenate([queries[0, :, cols].astype(jnp.float32), queries[1, :, cols].astype(jnp.float32)], axis=0)
        for j in range(2):
            h = p * 2 + j
            nope = both[:, 192 * j : 192 * j + 128].astype(jnp.bfloat16)
            rope = both[:, 192 * j + 128 : 192 * j + 192].astype(jnp.bfloat16)
            rows = pl.ds(pl.multiple_of(h * 16, 16), 16)
            q_all[rows, :512] = jnp.dot(nope, uk_v[h], preferred_element_type=jnp.float32).astype(jnp.bfloat16)
            q_all[rows, 512:] = rope
        return carry

    lax.fori_loop(0, head_count // 2, head_pair, 0)

    total = row_of.shape[0]
    block_here = jnp.int32(0)
    for b in range(8):
        block_here = block_here + jnp.where(decode_perm[b] == me, b, 0)
    sample = block_here * 8 + lax.broadcasted_iota(jnp.int32, (total, 128), 0) % 8
    prompt = jnp.zeros((total, 128), jnp.int32)
    ends = jnp.int32(0)
    for p in range(prompts):
        ends = ends + counts[p]
        prompt = prompt + jnp.where(sample >= ends, 1, 0)
    rows_vec = jnp.zeros((total, 128), jnp.int32)
    for p in range(prompts):
        rows_vec = jnp.where(prompt == p, prompt_rows[p], rows_vec)
    row_of[...] = rows_vec
    loads[2].wait()

    score_scale = (NOPE_DIM + ROPE_DIM) ** (-0.5)

    def begin():
        fresh = contrib[me].astype(jnp.float32)
        for k in range(1, 8):
            src = (me + k) % 8
            pltpu.make_async_copy(tokens.at[src], tokens.at[src], tok_recv.at[src]).wait()
            fresh = fresh + tokens[src].astype(jnp.float32)
        rope = fresh[:, 512:]
        swap = lax.broadcasted_iota(jnp.int32, (64, 64), 0) == (lax.broadcasted_iota(jnp.int32, (64, 64), 1) + 32) % 64
        swapped = jnp.dot(
            rope.astype(jnp.bfloat16), jnp.where(swap, 1.0, 0.0).astype(jnp.bfloat16), preferred_element_type=jnp.float32
        )
        new_keys[:, :512] = fresh[:, :512].astype(jnp.bfloat16)
        new_keys[:, 512:] = (rope * rope_cos[...] + swapped * rope_sin[...]).astype(jnp.bfloat16)
        scores = contract_last(q_all[...], new_keys[...]) * score_scale
        row = lax.broadcasted_iota(jnp.int32, (total, 16), 0) % 16
        key = lax.broadcasted_iota(jnp.int32, (total, 16), 1)
        seen = (row % 8 == key % 8) & (key // 8 <= row // 8)
        scores = jnp.where(seen, scores, masked_fill)
        top = jnp.max(scores, axis=1, keepdims=True)
        probs = jnp.exp(scores - top)
        m_ref[...] = jnp.broadcast_to(top, m_ref.shape)
        l_ref[...] = jnp.broadcast_to(jnp.sum(probs, axis=1, keepdims=True), l_ref.shape)
        acc[...] = jnp.dot(probs.astype(jnp.bfloat16), new_keys[:, :512], preferred_element_type=jnp.float32)

    def attend(src):
        keys = kv[src].reshape(prompts * block, kv.shape[-1])
        scores = contract_last(q_all[...], keys)
        rows = row_of[...]
        chosen = scores[:, :block]
        for r in range(1, prompts):
            chosen = jnp.where(rows == r, scores[:, r * block : (r + 1) * block], chosen)
        chosen = chosen * score_scale
        before = m_ref[...]
        top = jnp.maximum(before, jnp.max(chosen, axis=1, keepdims=True))
        fade = jnp.exp(before - top)
        probs = jnp.exp(chosen - top)
        m_ref[...] = top
        l_ref[...] = l_ref[...] * fade + jnp.sum(probs, axis=1, keepdims=True)
        spread = jnp.concatenate([jnp.where(rows == r, probs, 0.0).astype(jnp.bfloat16) for r in range(prompts)], axis=1)
        gained = jnp.dot(spread, keys[:, :512], preferred_element_type=jnp.float32)
        acc[...] = acc[...] * jnp.concatenate([fade] * 4, axis=1) + gained

    def turn(i, carry):
        @pl.when(i <= last)
        def _():
            await_block(layer(i) * 2 + y, core)

            @pl.when(z_goes_on(i))
            def _():
                z_copy(i).start()

            y_copy(i).start()
            sib_copy(i, y).start()

        @pl.when(i <= last + 1)
        def _():
            await_block(layer(i - 1) * 2 + flip, core)
            sib_copy(i - 1, flip).start()

        @pl.when(i == 2)
        def _():
            begin()

        @pl.when(i >= 2)
        def _():
            near_layer = layer(i - 2)

            @pl.when(i > 2)
            def _():
                await_block(near_layer * 2 + y, 1 - core)

            await_block(near_layer * 2 + flip, 1 - core)

            def one(side, c):
                attend(near_layer * 2 + side)
                return c

            lax.fori_loop(0, 2, one, 0)

        return carry

    lax.fori_loop(1, last + 3, turn, 0)

    att[...] = (acc[...] / jnp.concatenate([l_ref[...]] * 4, axis=1)).astype(jnp.bfloat16)
    loads[3].wait()

    def up_value(h, carry):
        got = jnp.dot(att[pl.ds(pl.multiple_of(h * 16, 16), 16), :], uv_v[h], preferred_element_type=jnp.float32)
        heads_all[me, :, pl.ds(pl.multiple_of(h * 128, 128), 128)] = got.astype(jnp.bfloat16)
        return carry

    lax.fori_loop(0, head_count, up_value, 0)

    def ho_copy(src, send, device):
        return remote(heads_all.at[src], heads_all.at[src], send, ho_recv.at[src], device)

    def ho_own(step):
        return ho_copy(me, ho_own_send.at[0 if step < 0 else 1], to(me + 2 * step))

    def ho_z(i):
        step = jnp.where(layer(i) < z, 2, -2)
        return ho_copy(layer(i) * 2 + y, ho_z_send.at[i], to(me + step))

    def ho_y(i):
        return ho_copy(layer(i) * 2 + y, ho_y_send.at[i], to(z * 2 + flip))

    def await_heads(src):
        pltpu.make_async_copy(heads_all.at[src], heads_all.at[src], ho_recv.at[src]).wait()

    ho_y(0).start()

    @pl.when(z < last)
    def _():
        ho_own(1).start()

    @pl.when(z > 0)
    def _():
        ho_own(-1).start()

    for i in range(1, last + 1):
        await_heads(layer(i) * 2 + y)

        @pl.when(z_goes_on(i))
        def _():
            ho_z(i).start()

        ho_y(i).start()
    for i in range(last + 1):
        await_heads(layer(i) * 2 + flip)
    loads[4].wait()

    depth = 512
    rows_out = part.shape[0]
    part[...] = jnp.zeros_like(part)

    def project(k, carry):
        cols = pl.ds(pl.multiple_of(k * depth, depth), depth)
        left = heads_all[:, :, cols].reshape(rows_out, depth)
        part[...] += jnp.dot(left, wout_v[cols, :], preferred_element_type=jnp.float32)
        return carry

    lax.fori_loop(0, wout_v.shape[0] // depth, project, 0)

    kept = rows_out // 2
    swap_copy = remote(
        part.at[pl.ds(pl.multiple_of((1 - core) * kept, kept), kept)], other, ex_sem.at[0], ex_sem.at[1], sibling
    )
    swap_copy.start()

    own_y_copy().wait_send()
    ho_y(0).wait_send()

    @pl.when(z < last)
    def _():
        own_copy(1).wait_send()
        ho_own(1).wait_send()

    @pl.when(z > 0)
    def _():
        own_copy(-1).wait_send()
        ho_own(-1).wait_send()

    sib_copy(0, flip).wait_send()
    for i in range(1, last + 1):

        @pl.when(z_goes_on(i))
        def _():
            z_copy(i).wait_send()
            ho_z(i).wait_send()

        y_copy(i).wait_send()
        ho_y(i).wait_send()
        sib_copy(i, y).wait_send()
        sib_copy(i, flip).wait_send()
    for k in range(1, 8):
        tok_copy(k).wait_send()
    swap_copy.wait()
    out[...] = part[pl.ds(pl.multiple_of(core * kept, kept), kept), :] + other[...]


def rope_tables(first, step_count, slots):
    half_dim = ROPE_DIM // 2
    freqs = np.float32(rope_base) ** (-np.arange(half_dim, dtype=np.float32) / np.float32(half_dim))
    angles = (first + np.arange(step_count)).astype(np.float32)[:, None] * freqs.astype(np.float32)[None, :]
    cosine = np.cos(angles.astype(np.float64)).astype(np.float32)
    sine = np.sin(angles.astype(np.float64)).astype(np.float32)
    return (
        np.repeat(np.concatenate([cosine, cosine], axis=1), slots, axis=0),
        np.repeat(np.concatenate([-sine, sine], axis=1), slots, axis=0),
    )


def fused_shards(store, queries, table, w_uk, w_uv, w_out, counts, prompt_rows, decode_perm, token_ids):
    roll_count = lax.axis_size("roll")
    step_count, slots_dev = queries.shape[:2]
    prompts, block, latent = store.shape
    head_count = w_uk.shape[0]
    rows_q = head_count * step_count * slots_dev
    rows_out = roll_count * step_count * slots_dev
    width = w_out.shape[1]
    cos_rows, sin_rows = rope_tables(block * roll_count, step_count, slots_dev)
    bf16, f32 = jnp.bfloat16, jnp.float32
    smem = pl.BlockSpec(memory_space=pltpu.SMEM)
    vmem = pl.BlockSpec(memory_space=pltpu.VMEM)
    anywhere = pl.BlockSpec(memory_space=pl.ANY)
    dma = pltpu.SemaphoreType.DMA
    summed = pl.pallas_call(
        fused_kernel,
        out_shape=jax.ShapeDtypeStruct((rows_out // 2, width), f32),
        in_specs=[smem, smem, smem, vmem, vmem, vmem, vmem] + [anywhere] * 5,
        out_specs=vmem,
        scratch_shapes=[
            pltpu.VMEM((roll_count, prompts, block, latent), bf16),
            pltpu.VMEM(table.shape, bf16),
            pltpu.VMEM(w_uk.shape, bf16),
            pltpu.VMEM(w_uv.shape, bf16),
            pltpu.VMEM(w_out.shape, bf16),
            pltpu.VMEM((roll_count, 16, latent), bf16),
            pltpu.VMEM((roll_count, 16, latent), bf16),
            pltpu.VMEM((16, latent), bf16),
            pltpu.VMEM((rows_q, latent), bf16),
            pltpu.VMEM((rows_q, 128), jnp.int32),
            pltpu.VMEM((rows_q, 128), f32),
            pltpu.VMEM((rows_q, 128), f32),
            pltpu.VMEM((rows_q, KV_RANK), f32),
            pltpu.VMEM((rows_q, KV_RANK), bf16),
            pltpu.VMEM((roll_count, 16, w_out.shape[0]), bf16),
            pltpu.VMEM((rows_out, width), f32),
            pltpu.VMEM((rows_out // 2, width), f32),
            dma((5,)), dma((8, 2)), dma((2,)), dma((4,)), dma((4,)), dma((4, 2)), dma((8,)), dma((8,)),
            dma((8,)), dma((2,)), dma((4,)), dma((4,)), dma((2,)),
        ],
        compiler_params=pltpu.CompilerParams(
            collective_id=0, has_side_effects=True, vmem_limit_bytes=56 * 1024 * 1024
        ),
        name="fused_attention",
    )(
        counts, prompt_rows, decode_perm, token_ids, jnp.asarray(cos_rows), jnp.asarray(sin_rows), queries, store, table,
        w_uk, w_uv, w_out,
    )
    by_slot = summed.reshape(-1, step_count, slots_dev, width).transpose(0, 2, 1, 3)
    return by_slot.reshape(-1, step_count, width).astype(bf16)


def solution(mesh):
    body = fused_shards if mesh.shape["roll"] == 8 and mesh.shape["head"] == 2 else shards
    in_specs = (
        P("grp", "roll", None),
        P(None, ("grp", "roll"), "head"),
        P("roll", None),
        P("head", None, None),
        P("head", None, None),
        P("head", "roll"),
        P("grp"),
        P("grp"),
        P("grp"),
        P("grp", None),
    )
    out_specs = P(("grp", "head"), None, "roll")
    return jax.shard_map(body, mesh=mesh, in_specs=in_specs, out_specs=out_specs, check_vma=False)
```

```python
import functools

import jax
import jax.numpy as jnp
import numpy as np
from jax import lax
from jax.experimental import pallas as pl
from jax.experimental.pallas import tpu as pltpu
from jax.sharding import PartitionSpec as P

KV_RANK = 512
ROPE_DIM = 64
NOPE_DIM = 128


masked_fill = -1e30
rope_base = 10000.0


def pick_values(values, positions):
    matches = positions[..., None] == jnp.arange(values.shape[0], dtype=jnp.int32)
    return jnp.sum(jnp.where(matches, values, 0), axis=-1)


def rotate_rope(latent_rows, positions):
    half_dim = ROPE_DIM // 2
    freqs = rope_base ** (-jnp.arange(half_dim, dtype=jnp.float32) / half_dim)
    angles = positions[:, None] * freqs[None, :]
    cosine = jnp.cos(angles)
    sine = jnp.sin(angles)
    front = latent_rows[..., KV_RANK : KV_RANK + half_dim]
    behind = latent_rows[..., KV_RANK + half_dim :]
    return jnp.concatenate(
        [
            latent_rows[..., :KV_RANK],
            front * cosine - behind * sine,
            front * sine + behind * cosine,
        ],
        axis=-1,
    )


def shards(store, queries, table, w_uk, w_uv, w_out, counts, prompt_rows, decode_perm, token_ids):
    roll_count = lax.axis_size("roll")
    roll_index = lax.axis_index("roll")
    step_count = queries.shape[0]
    slots_dev = queries.shape[1]
    latent_width = store.shape[2]
    cache_len = store.shape[1] * roll_count
    bound_ends = jnp.cumsum(counts)
    sample_ids = jnp.arange(roll_count * slots_dev, dtype=jnp.int32)
    prompt_of = jnp.sum((bound_ends[None, :] <= sample_ids[:, None]).astype(jnp.int32), axis=1)
    devices = jnp.arange(roll_count, dtype=jnp.int32)
    block_of = jnp.sum(
        jnp.where(decode_perm[None, :] == devices[:, None], devices[None, :], 0), axis=1
    )
    slot_offsets = jnp.arange(slots_dev, dtype=jnp.int32)
    slot_prompt = pick_values(prompt_of, block_of[:, None] * slots_dev + slot_offsets[None, :])
    send_rows = pick_values(prompt_rows, slot_prompt).reshape(-1)
    outgoing = jnp.take(store, send_rows, axis=0).reshape(
        roll_count, slots_dev, store.shape[1], latent_width
    )
    incoming = lax.all_to_all(outgoing, "roll", split_axis=0, concat_axis=2, tiled=True)
    cache_rows = incoming.reshape(slots_dev, cache_len, latent_width)
    flat_ids = token_ids.reshape(-1)
    vocab_dev = table.shape[0]
    vocab_base = roll_index * vocab_dev
    one_hot = (
        flat_ids[:, None] - vocab_base == jnp.arange(vocab_dev, dtype=jnp.int32)[None, :]
    ).astype(jnp.bfloat16)
    looked = lax.psum_scatter(
        jnp.dot(one_hot, table, preferred_element_type=jnp.float32),
        "roll",
        scatter_dimension=0,
        tiled=True,
    )
    looked = (
        looked.astype(jnp.bfloat16).astype(jnp.float32).reshape(slots_dev, step_count, latent_width)
    )
    positions = (cache_len + jnp.arange(step_count)).astype(jnp.float32)
    new_latents = rotate_rope(looked, positions).astype(jnp.bfloat16)
    head_count = w_uk.shape[0]
    query_parts = queries.reshape(step_count, slots_dev, head_count, -1)
    q_latent = jnp.einsum(
        "tshd,hdc->tshc", query_parts[..., :NOPE_DIM], w_uk, preferred_element_type=jnp.float32
    ).astype(jnp.bfloat16)
    q_full = jnp.concatenate([q_latent, query_parts[..., NOPE_DIM:]], axis=-1)
    score_scale = (NOPE_DIM + ROPE_DIM) ** (-0.5)
    cache_scores = (
        jnp.einsum("tshc,sjc->tshj", q_full, cache_rows, preferred_element_type=jnp.float32)
        * score_scale
    )
    new_scores = (
        jnp.einsum("tshc,suc->tshu", q_full, new_latents, preferred_element_type=jnp.float32)
        * score_scale
    )
    allowed = jnp.arange(step_count)[None, :] <= jnp.arange(step_count)[:, None]
    new_scores = jnp.where(allowed[:, None, None, :], new_scores, masked_fill)
    row_max = jnp.maximum(jnp.max(cache_scores, axis=-1), jnp.max(new_scores, axis=-1))[..., None]
    cache_exp = jnp.exp(cache_scores - row_max)
    new_exp = jnp.exp(new_scores - row_max)
    denom = jnp.sum(cache_exp, axis=-1, keepdims=True) + jnp.sum(new_exp, axis=-1, keepdims=True)
    cache_probs = (cache_exp / denom).astype(jnp.bfloat16)
    new_probs = (new_exp / denom).astype(jnp.bfloat16)
    attended = jnp.einsum(
        "tshj,sjc->tshc", cache_probs, cache_rows[..., :KV_RANK], preferred_element_type=jnp.float32
    )
    attended = attended + jnp.einsum(
        "tshu,suc->tshc", new_probs, new_latents[..., :KV_RANK], preferred_element_type=jnp.float32
    )
    attended = attended.astype(jnp.bfloat16)
    head_out = jnp.einsum(
        "tshc,hcv->tshv", attended, w_uv, preferred_element_type=jnp.float32
    ).astype(jnp.bfloat16)
    slot_major = head_out.transpose(1, 0, 2, 3).reshape(slots_dev * step_count, -1)
    partial_out = jnp.dot(
        lax.all_gather(slot_major, "roll", axis=0, tiled=True),
        w_out,
        preferred_element_type=jnp.float32,
    )
    summed = lax.psum_scatter(partial_out, "head", scatter_dimension=0, tiled=True)
    return summed.astype(jnp.bfloat16).reshape(-1, step_count, w_out.shape[1])


def contract_last(a, b):
    return lax.dot_general(a, b, (((1,), (1,)), ((), ())), preferred_element_type=jnp.float32)


def fused_kernel(
    counts, prompt_rows, decode_perm, token_ids, rope_cos, rope_sin, queries, store, table, w_uk, w_uv, w_out,
    out,
    kv, table_v, uk_v, uv_v, wout_v, contrib, tokens, new_keys, q_all, row_of, m_ref, l_ref, acc, att, heads_all, part, other,
    load_sem, kv_recv, own_send, z_send, y_send, sib_send, tok_recv, tok_send,
    ho_recv, ho_own_send, ho_z_send, ho_y_send, ex_sem,
):
    me = lax.axis_index("roll")
    core = lax.axis_index("head")
    z, y = me // 2, me % 2
    flip = 1 - y
    prompts = store.shape[0]
    half = prompts // 2
    block = store.shape[2]
    head_count = uk_v.shape[0]
    last = 3

    def to(roll):
        return {"roll": roll}

    sibling = {"head": 1 - core}
    mine = pl.ds(half * core, half)

    def remote(src, dst, send, recv, device):
        return pltpu.make_async_remote_copy(
            src_ref=src, dst_ref=dst, send_sem=send, recv_sem=recv, device_id=device,
            device_id_type=pl.DeviceIdType.MESH,
        )

    loads = [
        pltpu.make_async_copy(table, table_v, load_sem.at[0]),
        pltpu.make_async_copy(w_uk, uk_v, load_sem.at[1]),
        pltpu.make_async_copy(store, kv.at[me], load_sem.at[2]),
        pltpu.make_async_copy(w_uv, uv_v, load_sem.at[3]),
        pltpu.make_async_copy(w_out, wout_v, load_sem.at[4]),
    ]
    for load in loads:
        load.start()

    barrier = pltpu.get_barrier_semaphore()
    for k in range(1, 8):
        pl.semaphore_signal(barrier, inc=1, device_id=to((me + k) % 8), device_id_type=pl.DeviceIdType.MESH)
    pl.semaphore_signal(barrier, inc=1, device_id=sibling, device_id_type=pl.DeviceIdType.MESH)
    pl.semaphore_wait(barrier, 8)

    near = jnp.minimum(z, last - z)

    def layer(i):
        up = jnp.where(i == 0, near, jnp.where(i > near, i, i - 1))
        return jnp.where(z <= 1, up, last - up)

    own_block = store.at[mine]

    def own_copy(step):
        slot = 0 if step < 0 else 1
        return remote(own_block, kv.at[me, mine], own_send.at[slot], kv_recv.at[me, core], to(me + 2 * step))

    def z_copy(i):
        src = layer(i) * 2 + y
        step = jnp.where(layer(i) < z, 2, -2)
        return remote(kv.at[src, mine], kv.at[src, mine], z_send.at[i], kv_recv.at[src, core], to(me + step))

    def z_goes_on(i):
        return jnp.where(layer(i) < z, z < last, z > 0)

    def y_copy(i):
        src = layer(i) * 2 + y
        return remote(kv.at[src, mine], kv.at[src, mine], y_send.at[i], kv_recv.at[src, core], to(z * 2 + flip))

    def own_y_copy():
        return remote(own_block, kv.at[me, mine], y_send.at[0], kv_recv.at[me, core], to(z * 2 + flip))

    def sib_copy(i, side):
        src = layer(i) * 2 + side
        return remote(kv.at[src, mine], kv.at[src, mine], sib_send.at[i, side], kv_recv.at[src, core], sibling)

    def await_block(src, which):
        ref = kv.at[src, pl.ds(half * which, half)]
        pltpu.make_async_copy(ref, ref, kv_recv.at[src, which]).wait()

    own_y_copy().start()

    @pl.when(z < last)
    def _():
        own_copy(1).start()

    @pl.when(z > 0)
    def _():
        own_copy(-1).start()

    loads[0].wait()
    rows_here = table_v.shape[1]
    slots = token_ids.shape[1]
    ids = jnp.concatenate([token_ids[0:1, :], token_ids[1:2, :]], axis=1)
    spots = lax.broadcasted_iota(jnp.int32, (rows_here, 2 * slots), 0) + me * rows_here
    hot = jnp.where(ids == spots, 1.0, 0.0).astype(jnp.bfloat16)
    got = jnp.dot(table_v[...], hot, preferred_element_type=jnp.float32)
    picked = [got.T[t * slots : (t + 1) * slots].reshape(8, 8, got.shape[0]) for t in range(2)]
    contrib[...] = jnp.concatenate(picked, axis=1).astype(jnp.bfloat16)

    def tok_copy(k):
        dst = (me + k) % 8
        return remote(contrib.at[dst], tokens.at[me], tok_send.at[dst], tok_recv.at[me], to(dst))

    for k in range(1, 8):
        tok_copy(k).start()

    loads[1].wait()

    def head_pair(p, carry):
        cols = pl.ds(pl.multiple_of(p * 384, 128), 384)
        both = jnp.concatenate([queries[0, :, cols].astype(jnp.float32), queries[1, :, cols].astype(jnp.float32)], axis=0)
        for j in range(2):
            h = p * 2 + j
            nope = both[:, 192 * j : 192 * j + 128].astype(jnp.bfloat16)
            rope = both[:, 192 * j + 128 : 192 * j + 192].astype(jnp.bfloat16)
            rows = pl.ds(pl.multiple_of(h * 16, 16), 16)
            q_all[rows, :512] = jnp.dot(nope, uk_v[h], preferred_element_type=jnp.float32).astype(jnp.bfloat16)
            q_all[rows, 512:] = rope
        return carry

    lax.fori_loop(0, head_count // 2, head_pair, 0)

    total = row_of.shape[0]
    block_here = jnp.int32(0)
    for b in range(8):
        block_here = block_here + jnp.where(decode_perm[b] == me, b, 0)
    sample = block_here * 8 + lax.broadcasted_iota(jnp.int32, (total, 128), 0) % 8
    prompt = jnp.zeros((total, 128), jnp.int32)
    ends = jnp.int32(0)
    for p in range(prompts):
        ends = ends + counts[p]
        prompt = prompt + jnp.where(sample >= ends, 1, 0)
    rows_vec = jnp.zeros((total, 128), jnp.int32)
    for p in range(prompts):
        rows_vec = jnp.where(prompt == p, prompt_rows[p], rows_vec)
    row_of[...] = rows_vec
    loads[2].wait()

    score_scale = (NOPE_DIM + ROPE_DIM) ** (-0.5)

    def begin():
        fresh = contrib[me].astype(jnp.float32)
        for k in range(1, 8):
            src = (me + k) % 8
            pltpu.make_async_copy(tokens.at[src], tokens.at[src], tok_recv.at[src]).wait()
            fresh = fresh + tokens[src].astype(jnp.float32)
        rope = fresh[:, 512:]
        swap = lax.broadcasted_iota(jnp.int32, (64, 64), 0) == (lax.broadcasted_iota(jnp.int32, (64, 64), 1) + 32) % 64
        swapped = jnp.dot(
            rope.astype(jnp.bfloat16), jnp.where(swap, 1.0, 0.0).astype(jnp.bfloat16), preferred_element_type=jnp.float32
        )
        new_keys[:, :512] = fresh[:, :512].astype(jnp.bfloat16)
        new_keys[:, 512:] = (rope * rope_cos[...] + swapped * rope_sin[...]).astype(jnp.bfloat16)
        scores = contract_last(q_all[...], new_keys[...]) * score_scale
        row = lax.broadcasted_iota(jnp.int32, (total, 16), 0) % 16
        key = lax.broadcasted_iota(jnp.int32, (total, 16), 1)
        seen = (row % 8 == key % 8) & (key // 8 <= row // 8)
        scores = jnp.where(seen, scores, masked_fill)
        top = jnp.max(scores, axis=1, keepdims=True)
        probs = jnp.exp(scores - top)
        m_ref[...] = jnp.broadcast_to(top, m_ref.shape)
        l_ref[...] = jnp.broadcast_to(jnp.sum(probs, axis=1, keepdims=True), l_ref.shape)
        acc[...] = jnp.dot(probs.astype(jnp.bfloat16), new_keys[:, :512], preferred_element_type=jnp.float32)

    def attend(src):
        keys = jnp.concatenate([kv[src, r] for r in range(prompts)], axis=1)
        scores = jnp.dot(q_all[...], keys, preferred_element_type=jnp.float32)
        rows = row_of[...]
        chosen = scores[:, :block]
        for r in range(1, prompts):
            chosen = jnp.where(rows == r, scores[:, r * block : (r + 1) * block], chosen)
        chosen = chosen * score_scale
        before = m_ref[...]
        top = jnp.maximum(before, jnp.max(chosen, axis=1, keepdims=True))
        fade = jnp.exp(before - top)
        probs = jnp.exp(chosen - top)
        m_ref[...] = top
        l_ref[...] = l_ref[...] * fade + jnp.sum(probs, axis=1, keepdims=True)
        spread = jnp.concatenate([jnp.where(rows == r, probs, 0.0).astype(jnp.bfloat16) for r in range(prompts)], axis=1)
        gained = contract_last(spread, keys[:512])
        acc[...] = acc[...] * jnp.concatenate([fade] * 4, axis=1) + gained

    def turn(i, carry):
        @pl.when(i <= last)
        def _():
            await_block(layer(i) * 2 + y, core)

            @pl.when(z_goes_on(i))
            def _():
                z_copy(i).start()

            y_copy(i).start()
            sib_copy(i, y).start()

        @pl.when(i <= last + 1)
        def _():
            await_block(layer(i - 1) * 2 + flip, core)
            sib_copy(i - 1, flip).start()

        @pl.when(i == 2)
        def _():
            begin()

        @pl.when(i >= 2)
        def _():
            near_layer = layer(i - 2)

            @pl.when(i > 2)
            def _():
                await_block(near_layer * 2 + y, 1 - core)

            await_block(near_layer * 2 + flip, 1 - core)

            def one(side, c):
                attend(near_layer * 2 + side)
                return c

            lax.fori_loop(0, 2, one, 0)

        return carry

    lax.fori_loop(1, last + 3, turn, 0)

    att[...] = (acc[...] / jnp.concatenate([l_ref[...]] * 4, axis=1)).astype(jnp.bfloat16)
    loads[3].wait()

    def up_value(h, carry):
        got = jnp.dot(att[pl.ds(pl.multiple_of(h * 16, 16), 16), :], uv_v[h], preferred_element_type=jnp.float32)
        heads_all[me, :, pl.ds(pl.multiple_of(h * 128, 128), 128)] = got.astype(jnp.bfloat16)
        return carry

    lax.fori_loop(0, head_count, up_value, 0)

    def ho_copy(src, send, device):
        return remote(heads_all.at[src], heads_all.at[src], send, ho_recv.at[src], device)

    def ho_own(step):
        return ho_copy(me, ho_own_send.at[0 if step < 0 else 1], to(me + 2 * step))

    def ho_z(i):
        step = jnp.where(layer(i) < z, 2, -2)
        return ho_copy(layer(i) * 2 + y, ho_z_send.at[i], to(me + step))

    def ho_y(i):
        return ho_copy(layer(i) * 2 + y, ho_y_send.at[i], to(z * 2 + flip))

    def await_heads(src):
        pltpu.make_async_copy(heads_all.at[src], heads_all.at[src], ho_recv.at[src]).wait()

    ho_y(0).start()

    @pl.when(z < last)
    def _():
        ho_own(1).start()

    @pl.when(z > 0)
    def _():
        ho_own(-1).start()

    for i in range(1, last + 1):
        await_heads(layer(i) * 2 + y)

        @pl.when(z_goes_on(i))
        def _():
            ho_z(i).start()

        ho_y(i).start()
    for i in range(last + 1):
        await_heads(layer(i) * 2 + flip)
    loads[4].wait()

    depth = 512
    rows_out = part.shape[0]
    part[...] = jnp.zeros_like(part)

    def project(k, carry):
        cols = pl.ds(pl.multiple_of(k * depth, depth), depth)
        left = heads_all[:, :, cols].reshape(rows_out, depth)
        part[...] += jnp.dot(left, wout_v[cols, :], preferred_element_type=jnp.float32)
        return carry

    lax.fori_loop(0, wout_v.shape[0] // depth, project, 0)

    kept = rows_out // 2
    swap_copy = remote(
        part.at[pl.ds(pl.multiple_of((1 - core) * kept, kept), kept)], other, ex_sem.at[0], ex_sem.at[1], sibling
    )
    swap_copy.start()

    own_y_copy().wait_send()
    ho_y(0).wait_send()

    @pl.when(z < last)
    def _():
        own_copy(1).wait_send()
        ho_own(1).wait_send()

    @pl.when(z > 0)
    def _():
        own_copy(-1).wait_send()
        ho_own(-1).wait_send()

    sib_copy(0, flip).wait_send()
    for i in range(1, last + 1):

        @pl.when(z_goes_on(i))
        def _():
            z_copy(i).wait_send()
            ho_z(i).wait_send()

        y_copy(i).wait_send()
        ho_y(i).wait_send()
        sib_copy(i, y).wait_send()
        sib_copy(i, flip).wait_send()
    for k in range(1, 8):
        tok_copy(k).wait_send()
    swap_copy.wait()
    summed = part[pl.ds(pl.multiple_of(core * kept, kept), kept), :] + other[...]
    out[...] = summed.astype(out.dtype)


def rope_tables(first, step_count, slots):
    half_dim = ROPE_DIM // 2
    freqs = np.float32(rope_base) ** (-np.arange(half_dim, dtype=np.float32) / np.float32(half_dim))
    angles = (first + np.arange(step_count)).astype(np.float32)[:, None] * freqs.astype(np.float32)[None, :]
    cosine = np.cos(angles.astype(np.float64)).astype(np.float32)
    sine = np.sin(angles.astype(np.float64)).astype(np.float32)
    return (
        np.repeat(np.concatenate([cosine, cosine], axis=1), slots, axis=0),
        np.repeat(np.concatenate([-sine, sine], axis=1), slots, axis=0),
    )


def fused_shards(store, queries, table, w_uk, w_uv, w_out, counts, prompt_rows, decode_perm, token_ids):
    roll_count = lax.axis_size("roll")
    step_count, slots_dev = queries.shape[:2]
    prompts, block, latent = store.shape
    head_count = w_uk.shape[0]
    rows_q = head_count * step_count * slots_dev
    rows_out = roll_count * step_count * slots_dev
    width = w_out.shape[1]
    cos_rows, sin_rows = rope_tables(block * roll_count, step_count, slots_dev)
    bf16, f32 = jnp.bfloat16, jnp.float32
    smem = pl.BlockSpec(memory_space=pltpu.SMEM)
    vmem = pl.BlockSpec(memory_space=pltpu.VMEM)
    anywhere = pl.BlockSpec(memory_space=pl.ANY)
    dma = pltpu.SemaphoreType.DMA
    summed = pl.pallas_call(
        fused_kernel,
        out_shape=jax.ShapeDtypeStruct((rows_out // 2, width), bf16),
        in_specs=[smem, smem, smem, vmem, vmem, vmem, vmem] + [anywhere] * 5,
        out_specs=vmem,
        scratch_shapes=[
            pltpu.VMEM((roll_count, prompts, latent, block), bf16),
            pltpu.VMEM((latent, table.shape[0]), bf16),
            pltpu.VMEM(w_uk.shape, bf16),
            pltpu.VMEM(w_uv.shape, bf16),
            pltpu.VMEM(w_out.shape, bf16),
            pltpu.VMEM((roll_count, 16, latent), bf16),
            pltpu.VMEM((roll_count, 16, latent), bf16),
            pltpu.VMEM((16, latent), bf16),
            pltpu.VMEM((rows_q, latent), bf16),
            pltpu.VMEM((rows_q, 128), jnp.int32),
            pltpu.VMEM((rows_q, 128), f32),
            pltpu.VMEM((rows_q, 128), f32),
            pltpu.VMEM((rows_q, KV_RANK), f32),
            pltpu.VMEM((rows_q, KV_RANK), bf16),
            pltpu.VMEM((roll_count, 16, w_out.shape[0]), bf16),
            pltpu.VMEM((rows_out, width), f32),
            pltpu.VMEM((rows_out // 2, width), f32),
            dma((5,)), dma((8, 2)), dma((2,)), dma((4,)), dma((4,)), dma((4, 2)), dma((8,)), dma((8,)),
            dma((8,)), dma((2,)), dma((4,)), dma((4,)), dma((2,)),
        ],
        compiler_params=pltpu.CompilerParams(
            collective_id=0, has_side_effects=True, vmem_limit_bytes=56 * 1024 * 1024
        ),
        name="fused_attention",
    )(
        counts, prompt_rows, decode_perm, token_ids.T, jnp.asarray(cos_rows), jnp.asarray(sin_rows), queries,
        store.transpose(0, 2, 1), table.T, w_uk, w_uv, w_out,
    )
    by_slot = summed.reshape(-1, step_count, slots_dev, width).transpose(0, 2, 1, 3)
    return by_slot.reshape(-1, step_count, width)


def solution(mesh):
    body = fused_shards if mesh.shape["roll"] == 8 and mesh.shape["head"] == 2 else shards
    in_specs = (
        P("grp", "roll", None),
        P(None, ("grp", "roll"), "head"),
        P("roll", None),
        P("head", None, None),
        P("head", None, None),
        P("head", "roll"),
        P("grp"),
        P("grp"),
        P("grp"),
        P("grp", None),
    )
    out_specs = P(("grp", "head"), None, "roll")
    return jax.shard_map(body, mesh=mesh, in_specs=in_specs, out_specs=out_specs, check_vma=False)
```

```python
import functools

import jax
import jax.numpy as jnp
import numpy as np
from jax import lax
from jax.experimental import pallas as pl
from jax.experimental.pallas import tpu as pltpu
from jax.sharding import PartitionSpec as P

KV_RANK = 512
ROPE_DIM = 64
NOPE_DIM = 128


masked_fill = -1e30
rope_base = 10000.0


def pick_values(values, positions):
    matches = positions[..., None] == jnp.arange(values.shape[0], dtype=jnp.int32)
    return jnp.sum(jnp.where(matches, values, 0), axis=-1)


def rotate_rope(latent_rows, positions):
    half_dim = ROPE_DIM // 2
    freqs = rope_base ** (-jnp.arange(half_dim, dtype=jnp.float32) / half_dim)
    angles = positions[:, None] * freqs[None, :]
    cosine = jnp.cos(angles)
    sine = jnp.sin(angles)
    front = latent_rows[..., KV_RANK : KV_RANK + half_dim]
    behind = latent_rows[..., KV_RANK + half_dim :]
    return jnp.concatenate(
        [
            latent_rows[..., :KV_RANK],
            front * cosine - behind * sine,
            front * sine + behind * cosine,
        ],
        axis=-1,
    )


def shards(store, queries, table, w_uk, w_uv, w_out, counts, prompt_rows, decode_perm, token_ids):
    roll_count = lax.axis_size("roll")
    roll_index = lax.axis_index("roll")
    step_count = queries.shape[0]
    slots_dev = queries.shape[1]
    latent_width = store.shape[2]
    cache_len = store.shape[1] * roll_count
    bound_ends = jnp.cumsum(counts)
    sample_ids = jnp.arange(roll_count * slots_dev, dtype=jnp.int32)
    prompt_of = jnp.sum((bound_ends[None, :] <= sample_ids[:, None]).astype(jnp.int32), axis=1)
    devices = jnp.arange(roll_count, dtype=jnp.int32)
    block_of = jnp.sum(
        jnp.where(decode_perm[None, :] == devices[:, None], devices[None, :], 0), axis=1
    )
    slot_offsets = jnp.arange(slots_dev, dtype=jnp.int32)
    slot_prompt = pick_values(prompt_of, block_of[:, None] * slots_dev + slot_offsets[None, :])
    send_rows = pick_values(prompt_rows, slot_prompt).reshape(-1)
    outgoing = jnp.take(store, send_rows, axis=0).reshape(
        roll_count, slots_dev, store.shape[1], latent_width
    )
    incoming = lax.all_to_all(outgoing, "roll", split_axis=0, concat_axis=2, tiled=True)
    cache_rows = incoming.reshape(slots_dev, cache_len, latent_width)
    flat_ids = token_ids.reshape(-1)
    vocab_dev = table.shape[0]
    vocab_base = roll_index * vocab_dev
    one_hot = (
        flat_ids[:, None] - vocab_base == jnp.arange(vocab_dev, dtype=jnp.int32)[None, :]
    ).astype(jnp.bfloat16)
    looked = lax.psum_scatter(
        jnp.dot(one_hot, table, preferred_element_type=jnp.float32),
        "roll",
        scatter_dimension=0,
        tiled=True,
    )
    looked = (
        looked.astype(jnp.bfloat16).astype(jnp.float32).reshape(slots_dev, step_count, latent_width)
    )
    positions = (cache_len + jnp.arange(step_count)).astype(jnp.float32)
    new_latents = rotate_rope(looked, positions).astype(jnp.bfloat16)
    head_count = w_uk.shape[0]
    query_parts = queries.reshape(step_count, slots_dev, head_count, -1)
    q_latent = jnp.einsum(
        "tshd,hdc->tshc", query_parts[..., :NOPE_DIM], w_uk, preferred_element_type=jnp.float32
    ).astype(jnp.bfloat16)
    q_full = jnp.concatenate([q_latent, query_parts[..., NOPE_DIM:]], axis=-1)
    score_scale = (NOPE_DIM + ROPE_DIM) ** (-0.5)
    cache_scores = (
        jnp.einsum("tshc,sjc->tshj", q_full, cache_rows, preferred_element_type=jnp.float32)
        * score_scale
    )
    new_scores = (
        jnp.einsum("tshc,suc->tshu", q_full, new_latents, preferred_element_type=jnp.float32)
        * score_scale
    )
    allowed = jnp.arange(step_count)[None, :] <= jnp.arange(step_count)[:, None]
    new_scores = jnp.where(allowed[:, None, None, :], new_scores, masked_fill)
    row_max = jnp.maximum(jnp.max(cache_scores, axis=-1), jnp.max(new_scores, axis=-1))[..., None]
    cache_exp = jnp.exp(cache_scores - row_max)
    new_exp = jnp.exp(new_scores - row_max)
    denom = jnp.sum(cache_exp, axis=-1, keepdims=True) + jnp.sum(new_exp, axis=-1, keepdims=True)
    cache_probs = (cache_exp / denom).astype(jnp.bfloat16)
    new_probs = (new_exp / denom).astype(jnp.bfloat16)
    attended = jnp.einsum(
        "tshj,sjc->tshc", cache_probs, cache_rows[..., :KV_RANK], preferred_element_type=jnp.float32
    )
    attended = attended + jnp.einsum(
        "tshu,suc->tshc", new_probs, new_latents[..., :KV_RANK], preferred_element_type=jnp.float32
    )
    attended = attended.astype(jnp.bfloat16)
    head_out = jnp.einsum(
        "tshc,hcv->tshv", attended, w_uv, preferred_element_type=jnp.float32
    ).astype(jnp.bfloat16)
    slot_major = head_out.transpose(1, 0, 2, 3).reshape(slots_dev * step_count, -1)
    partial_out = jnp.dot(
        lax.all_gather(slot_major, "roll", axis=0, tiled=True),
        w_out,
        preferred_element_type=jnp.float32,
    )
    summed = lax.psum_scatter(partial_out, "head", scatter_dimension=0, tiled=True)
    return summed.astype(jnp.bfloat16).reshape(-1, step_count, w_out.shape[1])


def contract_last(a, b):
    return lax.dot_general(a, b, (((1,), (1,)), ((), ())), preferred_element_type=jnp.float32)


def fused_kernel(
    counts, prompt_rows, decode_perm, token_ids, rope_cos, rope_sin, queries, store, table, w_uk, w_uv, w_out,
    out,
    kv, table_v, uk_v, uv_v, wout_v, contrib, tokens, new_keys, q_all, row_of, m_ref, l_ref, acc, att, heads_all, part, other,
    load_sem, kv_recv, kv_own, kv_z, kv_y, sib_own, sib_z, sib_y, tok_recv, tok_send,
    ho_recv, ho_own, ho_z, ho_y, ex_sem,
):
    me = lax.axis_index("roll")
    core = lax.axis_index("head")
    z, y = me // 2, me % 2
    flip = 1 - y
    prompts = store.shape[0]
    half = prompts // 2
    block = store.shape[2]
    head_count = uk_v.shape[0]
    last = 3

    def to(roll):
        return {"roll": roll}

    sibling = {"head": 1 - core}
    def remote(src, dst, send, recv, device):
        return pltpu.make_async_remote_copy(
            src_ref=src, dst_ref=dst, send_sem=send, recv_sem=recv, device_id=device,
            device_id_type=pl.DeviceIdType.MESH,
        )

    loads = [
        pltpu.make_async_copy(table, table_v, load_sem.at[0]),
        pltpu.make_async_copy(w_uk, uk_v, load_sem.at[1]),
        pltpu.make_async_copy(store, kv.at[me], load_sem.at[2]),
        pltpu.make_async_copy(w_uv, uv_v, load_sem.at[3]),
        pltpu.make_async_copy(w_out, wout_v, load_sem.at[4]),
    ]
    for load in loads:
        load.start()

    barrier = pltpu.get_barrier_semaphore()
    for k in range(1, 8):
        pl.semaphore_signal(barrier, inc=1, device_id=to((me + k) % 8), device_id_type=pl.DeviceIdType.MESH)
    pl.semaphore_signal(barrier, inc=1, device_id=sibling, device_id_type=pl.DeviceIdType.MESH)
    pl.semaphore_wait(barrier, 8)

    near = jnp.minimum(z, last - z)

    def layer(i):
        up = jnp.where(i == 0, near, jnp.where(i > near, i, i - 1))
        return jnp.where(z <= 1, up, last - up)

    def from_side(side, t):
        layers = z if side == 0 else last - z
        extra = t == 2 * layers
        away = jnp.minimum(t // 2, layers - 1) + 1
        origin = jnp.where(extra, flip, y) + 2 * (z - away if side == 0 else z + away)
        crossed = 2 * (z - away if side == 0 else z + away) + flip
        comes = (layers > 0) & (t <= 2 * layers)
        goes_on = comes & (z < last if side == 0 else z > 0)
        return origin, jnp.where(extra, 1, t % 2), comes, goes_on, t < 2 * layers - 1, crossed

    def onward(side):
        return to(me + 2 if side == 0 else me - 2)

    across = to(z * 2 + flip)

    class Relay:
        def __init__(self, piece, recv, own, along, over, swap=None):
            self.piece, self.recv, self.own, self.along, self.over, self.swap = piece, recv, own, along, over, swap

        def send(self, src, q, sem, device):
            return remote(self.piece(src, q), self.piece(src, q), sem, self.recv(src, q), device)

        def arrive(self, src, q):
            ref = self.piece(src, q)
            pltpu.make_async_copy(ref, ref, self.recv(src, q)).wait()

        def mine(self, q, act):
            act(self.send(me, q, self.own.at[2, q], across))
            for side in range(2):

                @pl.when(z < last if side == 0 else z > 0)
                def _():
                    act(self.send(me, q, self.own.at[side, q], onward(side)))

        def end_extra(self, act):
            for side in range(2):

                @pl.when(z == 0 if side == 0 else z == last)
                def _():
                    act(self.send(z * 2 + flip, 1, self.own.at[3, side], onward(side)))

        def along_turn(self, t):
            for side in range(2):
                src, q, comes, goes_on, crosses, _ = from_side(side, t)

                @pl.when(comes)
                def _():
                    self.arrive(src, q)

                    @pl.when(goes_on)
                    def _():
                        self.send(src, q, self.along.at[side, t], onward(side)).start()

                    @pl.when(crosses)
                    def _():
                        self.send(src, q, self.over.at[side, t], across).start()

                    if self.swap:
                        self.send(src, q, self.swap[1].at[side, t], sibling).start()

        def own_crossed(self, t):
            self.arrive(z * 2 + flip, t)
            if self.swap:
                self.send(z * 2 + flip, t, self.swap[0].at[t], sibling).start()

        def crossed_turn(self, t):
            for side in range(2):
                _, q, _, _, crosses, src = from_side(side, t)

                @pl.when(crosses)
                def _():
                    self.arrive(src, q)
                    if self.swap:
                        self.send(src, q, self.swap[2].at[side, t], sibling).start()

        def turn(self, t):
            self.along_turn(t)

            @pl.when(t < 2)
            def _():
                self.own_crossed(t)

            @pl.when(t == 1)
            def _():
                self.end_extra(lambda c: c.start())

            @pl.when(t >= 2)
            def _():
                self.crossed_turn(t - 2)

        def settle(self):
            def leave(c):
                c.wait_send()

            for q in range(2):
                self.mine(q, leave)
                if self.swap:
                    leave(self.send(z * 2 + flip, q, self.swap[0].at[q], sibling))
            self.end_extra(leave)

            def one(t, carry):
                for side in range(2):
                    src, q, comes, goes_on, crosses, other_src = from_side(side, t)

                    @pl.when(goes_on)
                    def _():
                        leave(self.send(src, q, self.along.at[side, t], onward(side)))

                    @pl.when(crosses)
                    def _():
                        leave(self.send(src, q, self.over.at[side, t], across))

                    if self.swap:

                        @pl.when(comes)
                        def _():
                            leave(self.send(src, q, self.swap[1].at[side, t], sibling))

                        @pl.when(crosses)
                        def _():
                            leave(self.send(other_src, q, self.swap[2].at[side, t], sibling))

                return carry

            lax.fori_loop(0, turns, one, 0)

    turns = 7
    cache = Relay(
        lambda src, q: kv.at[src, half * core + q],
        lambda src, q: kv_recv.at[src, half * core + q],
        kv_own, kv_z, kv_y, (sib_own, sib_z, sib_y),
    )

    def await_sibling(src):
        for q in range(half):
            r = half * (1 - core) + q
            pltpu.make_async_copy(kv.at[src, r], kv.at[src, r], kv_recv.at[src, r]).wait()

    def send_own_cache(q, act):
        own = store.at[half * core + q]
        here = kv.at[me, half * core + q]
        sem = kv_recv.at[me, half * core + q]
        act(remote(own, here, kv_own.at[2, q], sem, across))
        for side in range(2):

            @pl.when(z < last if side == 0 else z > 0)
            def _():
                act(remote(own, here, kv_own.at[side, q], sem, onward(side)))

    cache.mine = send_own_cache
    for q in range(2):
        cache.mine(q, lambda c: c.start())

    loads[0].wait()
    rows_here = table_v.shape[1]
    slots = token_ids.shape[1]
    ids = jnp.concatenate([token_ids[0:1, :], token_ids[1:2, :]], axis=1)
    spots = lax.broadcasted_iota(jnp.int32, (rows_here, 2 * slots), 0) + me * rows_here
    hot = jnp.where(ids == spots, 1.0, 0.0).astype(jnp.bfloat16)
    got = jnp.dot(table_v[...], hot, preferred_element_type=jnp.float32)
    picked = [got.T[t * slots : (t + 1) * slots].reshape(8, 8, got.shape[0]) for t in range(2)]
    contrib[...] = jnp.concatenate(picked, axis=1).astype(jnp.bfloat16)

    def tok_copy(k):
        dst = (me + k) % 8
        return remote(contrib.at[dst], tokens.at[me], tok_send.at[dst], tok_recv.at[me], to(dst))

    for k in range(1, 8):
        tok_copy(k).start()

    loads[1].wait()

    def head_pair(p, carry):
        cols = pl.ds(pl.multiple_of(p * 384, 128), 384)
        both = jnp.concatenate([queries[0, :, cols].astype(jnp.float32), queries[1, :, cols].astype(jnp.float32)], axis=0)
        for j in range(2):
            h = p * 2 + j
            nope = both[:, 192 * j : 192 * j + 128].astype(jnp.bfloat16)
            rope = both[:, 192 * j + 128 : 192 * j + 192].astype(jnp.bfloat16)
            rows = pl.ds(pl.multiple_of(h * 16, 16), 16)
            q_all[rows, :512] = jnp.dot(nope, uk_v[h], preferred_element_type=jnp.float32).astype(jnp.bfloat16)
            q_all[rows, 512:] = rope
        return carry

    total = row_of.shape[0]
    block_here = jnp.int32(0)
    for b in range(8):
        block_here = block_here + jnp.where(decode_perm[b] == me, b, 0)
    sample = block_here * 8 + lax.broadcasted_iota(jnp.int32, (total, 128), 0) % 8
    prompt = jnp.zeros((total, 128), jnp.int32)
    ends = jnp.int32(0)
    for p in range(prompts):
        ends = ends + counts[p]
        prompt = prompt + jnp.where(sample >= ends, 1, 0)
    rows_vec = jnp.zeros((total, 128), jnp.int32)
    for p in range(prompts):
        rows_vec = jnp.where(prompt == p, prompt_rows[p], rows_vec)
    row_of[...] = rows_vec
    loads[2].wait()

    score_scale = (NOPE_DIM + ROPE_DIM) ** (-0.5)

    def begin():
        fresh = contrib[me].astype(jnp.float32)
        for k in range(1, 8):
            src = (me + k) % 8
            pltpu.make_async_copy(tokens.at[src], tokens.at[src], tok_recv.at[src]).wait()
            fresh = fresh + tokens[src].astype(jnp.float32)
        rope = fresh[:, 512:]
        swap = lax.broadcasted_iota(jnp.int32, (64, 64), 0) == (lax.broadcasted_iota(jnp.int32, (64, 64), 1) + 32) % 64
        swapped = jnp.dot(
            rope.astype(jnp.bfloat16), jnp.where(swap, 1.0, 0.0).astype(jnp.bfloat16), preferred_element_type=jnp.float32
        )
        new_keys[:, :512] = fresh[:, :512].astype(jnp.bfloat16)
        new_keys[:, 512:] = (rope * rope_cos[...] + swapped * rope_sin[...]).astype(jnp.bfloat16)
        scores = contract_last(q_all[...], new_keys[...]) * score_scale
        row = lax.broadcasted_iota(jnp.int32, (total, 16), 0) % 16
        key = lax.broadcasted_iota(jnp.int32, (total, 16), 1)
        seen = (row % 8 == key % 8) & (key // 8 <= row // 8)
        scores = jnp.where(seen, scores, masked_fill)
        top = jnp.max(scores, axis=1, keepdims=True)
        probs = jnp.exp(scores - top)
        m_ref[...] = jnp.broadcast_to(top, m_ref.shape)
        l_ref[...] = jnp.broadcast_to(jnp.sum(probs, axis=1, keepdims=True), l_ref.shape)
        acc[...] = jnp.dot(probs.astype(jnp.bfloat16), new_keys[:, :512], preferred_element_type=jnp.float32)

    def attend(src):
        keys = jnp.concatenate([kv[src, r] for r in range(prompts)], axis=1)
        scores = jnp.dot(q_all[...], keys, preferred_element_type=jnp.float32)
        rows = row_of[...]
        chosen = scores[:, :block]
        for r in range(1, prompts):
            chosen = jnp.where(rows == r, scores[:, r * block : (r + 1) * block], chosen)
        chosen = chosen * score_scale
        before = m_ref[...]
        top = jnp.maximum(before, jnp.max(chosen, axis=1, keepdims=True))
        fade = jnp.exp(before - top)
        probs = jnp.exp(chosen - top)
        m_ref[...] = top
        l_ref[...] = l_ref[...] * fade + jnp.sum(probs, axis=1, keepdims=True)
        spread = jnp.concatenate([jnp.where(rows == r, probs, 0.0).astype(jnp.bfloat16) for r in range(prompts)], axis=1)
        gained = contract_last(spread, keys[:512])
        acc[...] = acc[...] * jnp.concatenate([fade] * 4, axis=1) + gained

    def gather_turn(t, carry):
        cache.turn(t)

        @pl.when(t < 2)
        def _():
            pairs = head_count // 4
            lax.fori_loop(t * pairs, t * pairs + pairs, head_pair, 0)

        @pl.when(t == 2)
        def _():
            begin()

        def one(j, c):
            k = 2 * t - 5 + j

            @pl.when((k >= 0) & (k < 8))
            def _():
                src = 2 * layer(k // 2) + jnp.where(k % 2 == 0, y, flip)

                @pl.when(k > 0)
                def _():
                    await_sibling(src)

                attend(src)

            return c

        @pl.when(t >= 2)
        def _():
            lax.fori_loop(0, 2, one, 0)

        return carry

    lax.fori_loop(0, turns, gather_turn, 0)

    att[...] = (acc[...] / jnp.concatenate([l_ref[...]] * 4, axis=1)).astype(jnp.bfloat16)
    loads[3].wait()

    per_piece = head_count // 2

    def up_value(h, carry):
        got = jnp.dot(att[pl.ds(pl.multiple_of(h * 16, 16), 16), :], uv_v[h], preferred_element_type=jnp.float32)
        spot = h % per_piece
        heads_all[h // per_piece, me, :, pl.ds(pl.multiple_of(spot * 128, 128), 128)] = got.astype(jnp.bfloat16)
        return carry

    shared = Relay(lambda src, q: heads_all.at[q, src], lambda src, q: ho_recv.at[src, q], ho_own, ho_z, ho_y)
    for q in range(2):
        lax.fori_loop(q * per_piece, (q + 1) * per_piece, up_value, 0)
        shared.mine(q, lambda c: c.start())

    def share_turn(t, carry):
        shared.turn(t)
        return carry

    lax.fori_loop(0, turns, share_turn, 0)
    loads[4].wait()

    depth = 512
    rows_out = part.shape[0]
    part[...] = jnp.zeros_like(part)
    per_half = wout_v.shape[0] // 2 // depth

    def project(k, carry):
        cols = pl.ds(pl.multiple_of((k % per_half) * depth, depth), depth)
        left = heads_all[k // per_half, :, :, cols].reshape(rows_out, depth)
        rows = pl.ds(pl.multiple_of(k * depth, depth), depth)
        part[...] += jnp.dot(left, wout_v[rows, :], preferred_element_type=jnp.float32)
        return carry

    lax.fori_loop(0, wout_v.shape[0] // depth, project, 0)

    kept = rows_out // 2
    swap_copy = remote(
        part.at[pl.ds(pl.multiple_of((1 - core) * kept, kept), kept)], other, ex_sem.at[0], ex_sem.at[1], sibling
    )
    swap_copy.start()

    cache.settle()
    shared.settle()
    for k in range(1, 8):
        tok_copy(k).wait_send()
    swap_copy.wait()
    summed = part[pl.ds(pl.multiple_of(core * kept, kept), kept), :] + other[...]
    out[...] = summed.astype(out.dtype)


def rope_tables(first, step_count, slots):
    half_dim = ROPE_DIM // 2
    freqs = np.float32(rope_base) ** (-np.arange(half_dim, dtype=np.float32) / np.float32(half_dim))
    angles = (first + np.arange(step_count)).astype(np.float32)[:, None] * freqs.astype(np.float32)[None, :]
    cosine = np.cos(angles.astype(np.float64)).astype(np.float32)
    sine = np.sin(angles.astype(np.float64)).astype(np.float32)
    return (
        np.repeat(np.concatenate([cosine, cosine], axis=1), slots, axis=0),
        np.repeat(np.concatenate([-sine, sine], axis=1), slots, axis=0),
    )


def fused_shards(store, queries, table, w_uk, w_uv, w_out, counts, prompt_rows, decode_perm, token_ids):
    roll_count = lax.axis_size("roll")
    step_count, slots_dev = queries.shape[:2]
    prompts, block, latent = store.shape
    head_count = w_uk.shape[0]
    rows_q = head_count * step_count * slots_dev
    rows_out = roll_count * step_count * slots_dev
    width = w_out.shape[1]
    cos_rows, sin_rows = rope_tables(block * roll_count, step_count, slots_dev)
    bf16, f32 = jnp.bfloat16, jnp.float32
    smem = pl.BlockSpec(memory_space=pltpu.SMEM)
    vmem = pl.BlockSpec(memory_space=pltpu.VMEM)
    anywhere = pl.BlockSpec(memory_space=pl.ANY)
    dma = pltpu.SemaphoreType.DMA
    summed = pl.pallas_call(
        fused_kernel,
        out_shape=jax.ShapeDtypeStruct((rows_out // 2, width), bf16),
        in_specs=[smem, smem, smem, vmem, vmem, vmem, vmem] + [anywhere] * 5,
        out_specs=vmem,
        scratch_shapes=[
            pltpu.VMEM((roll_count, prompts, latent, block), bf16),
            pltpu.VMEM((latent, table.shape[0]), bf16),
            pltpu.VMEM(w_uk.shape, bf16),
            pltpu.VMEM(w_uv.shape, bf16),
            pltpu.VMEM(w_out.shape, bf16),
            pltpu.VMEM((roll_count, 16, latent), bf16),
            pltpu.VMEM((roll_count, 16, latent), bf16),
            pltpu.VMEM((16, latent), bf16),
            pltpu.VMEM((rows_q, latent), bf16),
            pltpu.VMEM((rows_q, 128), jnp.int32),
            pltpu.VMEM((rows_q, 128), f32),
            pltpu.VMEM((rows_q, 128), f32),
            pltpu.VMEM((rows_q, KV_RANK), f32),
            pltpu.VMEM((rows_q, KV_RANK), bf16),
            pltpu.VMEM((2, roll_count, 16, w_out.shape[0] // 2), bf16),
            pltpu.VMEM((rows_out, width), f32),
            pltpu.VMEM((rows_out // 2, width), f32),
            dma((5,)), dma((8, 4)), dma((4, 2)), dma((2, 7)), dma((2, 7)), dma((2,)), dma((2, 7)), dma((2, 7)),
            dma((8,)), dma((8,)), dma((8, 2)), dma((4, 2)), dma((2, 7)), dma((2, 7)), dma((2,)),
        ],
        compiler_params=pltpu.CompilerParams(
            collective_id=0, has_side_effects=True, vmem_limit_bytes=56 * 1024 * 1024
        ),
        name="fused_attention",
    )(
        counts, prompt_rows, decode_perm, token_ids.T, jnp.asarray(cos_rows), jnp.asarray(sin_rows), queries,
        store.transpose(0, 2, 1), table.T, w_uk, w_uv, w_out,
    )
    by_slot = summed.reshape(-1, step_count, slots_dev, width).transpose(0, 2, 1, 3)
    return by_slot.reshape(-1, step_count, width)


def solution(mesh):
    body = fused_shards if mesh.shape["roll"] == 8 and mesh.shape["head"] == 2 else shards
    in_specs = (
        P("grp", "roll", None),
        P(None, ("grp", "roll"), "head"),
        P("roll", None),
        P("head", None, None),
        P("head", None, None),
        P("head", "roll"),
        P("grp"),
        P("grp"),
        P("grp"),
        P("grp", None),
    )
    out_specs = P(("grp", "head"), None, "roll")
    return jax.shard_map(body, mesh=mesh, in_specs=in_specs, out_specs=out_specs, check_vma=False)
```

```python
import functools

import jax
import jax.numpy as jnp
import numpy as np
from jax import lax
from jax.experimental import pallas as pl
from jax.experimental.pallas import tpu as pltpu
from jax.sharding import PartitionSpec as P

KV_RANK = 512
ROPE_DIM = 64
NOPE_DIM = 128


masked_fill = -1e30
rope_base = 10000.0


def pick_values(values, positions):
    matches = positions[..., None] == jnp.arange(values.shape[0], dtype=jnp.int32)
    return jnp.sum(jnp.where(matches, values, 0), axis=-1)


def rotate_rope(latent_rows, positions):
    half_dim = ROPE_DIM // 2
    freqs = rope_base ** (-jnp.arange(half_dim, dtype=jnp.float32) / half_dim)
    angles = positions[:, None] * freqs[None, :]
    cosine = jnp.cos(angles)
    sine = jnp.sin(angles)
    front = latent_rows[..., KV_RANK : KV_RANK + half_dim]
    behind = latent_rows[..., KV_RANK + half_dim :]
    return jnp.concatenate(
        [
            latent_rows[..., :KV_RANK],
            front * cosine - behind * sine,
            front * sine + behind * cosine,
        ],
        axis=-1,
    )


def shards(store, queries, table, w_uk, w_uv, w_out, counts, prompt_rows, decode_perm, token_ids):
    roll_count = lax.axis_size("roll")
    roll_index = lax.axis_index("roll")
    step_count = queries.shape[0]
    slots_dev = queries.shape[1]
    latent_width = store.shape[2]
    cache_len = store.shape[1] * roll_count
    bound_ends = jnp.cumsum(counts)
    sample_ids = jnp.arange(roll_count * slots_dev, dtype=jnp.int32)
    prompt_of = jnp.sum((bound_ends[None, :] <= sample_ids[:, None]).astype(jnp.int32), axis=1)
    devices = jnp.arange(roll_count, dtype=jnp.int32)
    block_of = jnp.sum(
        jnp.where(decode_perm[None, :] == devices[:, None], devices[None, :], 0), axis=1
    )
    slot_offsets = jnp.arange(slots_dev, dtype=jnp.int32)
    slot_prompt = pick_values(prompt_of, block_of[:, None] * slots_dev + slot_offsets[None, :])
    send_rows = pick_values(prompt_rows, slot_prompt).reshape(-1)
    outgoing = jnp.take(store, send_rows, axis=0).reshape(
        roll_count, slots_dev, store.shape[1], latent_width
    )
    incoming = lax.all_to_all(outgoing, "roll", split_axis=0, concat_axis=2, tiled=True)
    cache_rows = incoming.reshape(slots_dev, cache_len, latent_width)
    flat_ids = token_ids.reshape(-1)
    vocab_dev = table.shape[0]
    vocab_base = roll_index * vocab_dev
    one_hot = (
        flat_ids[:, None] - vocab_base == jnp.arange(vocab_dev, dtype=jnp.int32)[None, :]
    ).astype(jnp.bfloat16)
    looked = lax.psum_scatter(
        jnp.dot(one_hot, table, preferred_element_type=jnp.float32),
        "roll",
        scatter_dimension=0,
        tiled=True,
    )
    looked = (
        looked.astype(jnp.bfloat16).astype(jnp.float32).reshape(slots_dev, step_count, latent_width)
    )
    positions = (cache_len + jnp.arange(step_count)).astype(jnp.float32)
    new_latents = rotate_rope(looked, positions).astype(jnp.bfloat16)
    head_count = w_uk.shape[0]
    query_parts = queries.reshape(step_count, slots_dev, head_count, -1)
    q_latent = jnp.einsum(
        "tshd,hdc->tshc", query_parts[..., :NOPE_DIM], w_uk, preferred_element_type=jnp.float32
    ).astype(jnp.bfloat16)
    q_full = jnp.concatenate([q_latent, query_parts[..., NOPE_DIM:]], axis=-1)
    score_scale = (NOPE_DIM + ROPE_DIM) ** (-0.5)
    cache_scores = (
        jnp.einsum("tshc,sjc->tshj", q_full, cache_rows, preferred_element_type=jnp.float32)
        * score_scale
    )
    new_scores = (
        jnp.einsum("tshc,suc->tshu", q_full, new_latents, preferred_element_type=jnp.float32)
        * score_scale
    )
    allowed = jnp.arange(step_count)[None, :] <= jnp.arange(step_count)[:, None]
    new_scores = jnp.where(allowed[:, None, None, :], new_scores, masked_fill)
    row_max = jnp.maximum(jnp.max(cache_scores, axis=-1), jnp.max(new_scores, axis=-1))[..., None]
    cache_exp = jnp.exp(cache_scores - row_max)
    new_exp = jnp.exp(new_scores - row_max)
    denom = jnp.sum(cache_exp, axis=-1, keepdims=True) + jnp.sum(new_exp, axis=-1, keepdims=True)
    cache_probs = (cache_exp / denom).astype(jnp.bfloat16)
    new_probs = (new_exp / denom).astype(jnp.bfloat16)
    attended = jnp.einsum(
        "tshj,sjc->tshc", cache_probs, cache_rows[..., :KV_RANK], preferred_element_type=jnp.float32
    )
    attended = attended + jnp.einsum(
        "tshu,suc->tshc", new_probs, new_latents[..., :KV_RANK], preferred_element_type=jnp.float32
    )
    attended = attended.astype(jnp.bfloat16)
    head_out = jnp.einsum(
        "tshc,hcv->tshv", attended, w_uv, preferred_element_type=jnp.float32
    ).astype(jnp.bfloat16)
    slot_major = head_out.transpose(1, 0, 2, 3).reshape(slots_dev * step_count, -1)
    partial_out = jnp.dot(
        lax.all_gather(slot_major, "roll", axis=0, tiled=True),
        w_out,
        preferred_element_type=jnp.float32,
    )
    summed = lax.psum_scatter(partial_out, "head", scatter_dimension=0, tiled=True)
    return summed.astype(jnp.bfloat16).reshape(-1, step_count, w_out.shape[1])


def contract_last(a, b):
    return lax.dot_general(a, b, (((1,), (1,)), ((), ())), preferred_element_type=jnp.float32)


def fused_kernel(
    counts, prompt_rows, decode_perm, token_ids, rope_cos, rope_sin, queries, store, table, w_uk, w_uv, w_out,
    out,
    kv, table_v, uk_v, uv_v, wout_v, contrib, tokens, tok_in, tok_out, new_keys, q_all, row_of, m_ref, l_ref, acc, att, heads_all, part, other,
    load_sem, kv_recv, kv_own, kv_z, kv_y, sib_own, sib_z, sib_y, tok_recv, tok_send,
    ho_recv, ho_own, ho_z, ho_y, ex_sem,
):
    me = lax.axis_index("roll")
    core = lax.axis_index("head")
    z, y = me // 2, me % 2
    flip = 1 - y
    prompts = store.shape[0]
    half = prompts // 2
    block = store.shape[2]
    head_count = uk_v.shape[0]
    last = 3

    def to(roll):
        return {"roll": roll}

    sibling = {"head": 1 - core}
    def remote(src, dst, send, recv, device):
        return pltpu.make_async_remote_copy(
            src_ref=src, dst_ref=dst, send_sem=send, recv_sem=recv, device_id=device,
            device_id_type=pl.DeviceIdType.MESH,
        )

    loads = [
        pltpu.make_async_copy(table, table_v, load_sem.at[0]),
        pltpu.make_async_copy(w_uk, uk_v, load_sem.at[1]),
        pltpu.make_async_copy(store, kv.at[me], load_sem.at[2]),
        pltpu.make_async_copy(w_uv, uv_v, load_sem.at[3]),
        pltpu.make_async_copy(w_out, wout_v, load_sem.at[4]),
    ]
    for load in loads:
        load.start()

    barrier = pltpu.get_barrier_semaphore()
    def greet(device):
        pl.semaphore_signal(barrier, inc=1, device_id=device, device_id_type=pl.DeviceIdType.MESH)

    greet(to(z * 2 + flip))
    greet(sibling)

    @pl.when(z < last)
    def _():
        greet(to(me + 2))

    @pl.when(z > 0)
    def _():
        greet(to(me - 2))

    pl.semaphore_wait(barrier, 2 + jnp.where(z < last, 1, 0) + jnp.where(z > 0, 1, 0))

    near = jnp.minimum(z, last - z)

    def layer(i):
        up = jnp.where(i == 0, near, jnp.where(i > near, i, i - 1))
        return jnp.where(z <= 1, up, last - up)

    def from_side(side, t):
        layers = z if side == 0 else last - z
        extra = t == 2 * layers
        away = jnp.minimum(t // 2, layers - 1) + 1
        origin = jnp.where(extra, flip, y) + 2 * (z - away if side == 0 else z + away)
        crossed = 2 * (z - away if side == 0 else z + away) + flip
        comes = (layers > 0) & (t <= 2 * layers)
        goes_on = comes & (z < last if side == 0 else z > 0)
        return origin, jnp.where(extra, 1, t % 2), comes, goes_on, t < 2 * layers - 1, crossed

    def onward(side):
        return to(me + 2 if side == 0 else me - 2)

    across = to(z * 2 + flip)

    class Relay:
        def __init__(self, piece, recv, own, along, over, swap=None):
            self.piece, self.recv, self.own, self.along, self.over, self.swap = piece, recv, own, along, over, swap

        def send(self, src, q, sem, device):
            return remote(self.piece(src, q), self.piece(src, q), sem, self.recv(src, q), device)

        def arrive(self, src, q):
            ref = self.piece(src, q)
            pltpu.make_async_copy(ref, ref, self.recv(src, q)).wait()

        def mine(self, q, act):
            act(self.send(me, q, self.own.at[2, q], across))
            for side in range(2):

                @pl.when(z < last if side == 0 else z > 0)
                def _():
                    act(self.send(me, q, self.own.at[side, q], onward(side)))

        def end_extra(self, act):
            for side in range(2):

                @pl.when(z == 0 if side == 0 else z == last)
                def _():
                    act(self.send(z * 2 + flip, 1, self.own.at[3, side], onward(side)))

        def along_turn(self, t):
            for side in range(2):
                src, q, comes, goes_on, crosses, _ = from_side(side, t)

                @pl.when(comes)
                def _():
                    self.arrive(src, q)

                    @pl.when(goes_on)
                    def _():
                        self.send(src, q, self.along.at[side, t], onward(side)).start()

                    @pl.when(crosses)
                    def _():
                        self.send(src, q, self.over.at[side, t], across).start()

                    if self.swap:
                        self.send(src, q, self.swap[1].at[side, t], sibling).start()

        def own_crossed(self, t):
            self.arrive(z * 2 + flip, t)
            if self.swap:
                self.send(z * 2 + flip, t, self.swap[0].at[t], sibling).start()

        def crossed_turn(self, t):
            for side in range(2):
                _, q, _, _, crosses, src = from_side(side, t)

                @pl.when(crosses)
                def _():
                    self.arrive(src, q)
                    if self.swap:
                        self.send(src, q, self.swap[2].at[side, t], sibling).start()

        def turn(self, t):
            self.along_turn(t)

            @pl.when(t < 2)
            def _():
                self.own_crossed(t)

            @pl.when(t == 1)
            def _():
                self.end_extra(lambda c: c.start())

            @pl.when(t >= 2)
            def _():
                self.crossed_turn(t - 2)

        def settle(self):
            def leave(c):
                c.wait_send()

            for q in range(2):
                self.mine(q, leave)
                if self.swap:
                    leave(self.send(z * 2 + flip, q, self.swap[0].at[q], sibling))
            self.end_extra(leave)

            def one(t, carry):
                for side in range(2):
                    src, q, comes, goes_on, crosses, other_src = from_side(side, t)

                    @pl.when(goes_on)
                    def _():
                        leave(self.send(src, q, self.along.at[side, t], onward(side)))

                    @pl.when(crosses)
                    def _():
                        leave(self.send(src, q, self.over.at[side, t], across))

                    if self.swap:

                        @pl.when(comes)
                        def _():
                            leave(self.send(src, q, self.swap[1].at[side, t], sibling))

                        @pl.when(crosses)
                        def _():
                            leave(self.send(other_src, q, self.swap[2].at[side, t], sibling))

                return carry

            lax.fori_loop(0, turns, one, 0)

    turns = 7
    cache = Relay(
        lambda src, q: kv.at[src, half * core + q],
        lambda src, q: kv_recv.at[src, half * core + q],
        kv_own, kv_z, kv_y, (sib_own, sib_z, sib_y),
    )

    def await_sibling(src):
        for q in range(half):
            r = half * (1 - core) + q
            pltpu.make_async_copy(kv.at[src, r], kv.at[src, r], kv_recv.at[src, r]).wait()

    def send_own_cache(q, act):
        own = store.at[half * core + q]
        here = kv.at[me, half * core + q]
        sem = kv_recv.at[me, half * core + q]
        act(remote(own, here, kv_own.at[2, q], sem, across))
        for side in range(2):

            @pl.when(z < last if side == 0 else z > 0)
            def _():
                act(remote(own, here, kv_own.at[side, q], sem, onward(side)))

    cache.mine = send_own_cache
    for q in range(2):
        cache.mine(q, lambda c: c.start())

    loads[0].wait()
    rows_here = table_v.shape[1]
    slots = token_ids.shape[1]
    ids = jnp.concatenate([token_ids[0:1, :], token_ids[1:2, :]], axis=1)
    spots = lax.broadcasted_iota(jnp.int32, (rows_here, 2 * slots), 0) + me * rows_here
    hot = jnp.where(ids == spots, 1.0, 0.0).astype(jnp.bfloat16)
    got = jnp.dot(table_v[...], hot, preferred_element_type=jnp.float32)
    picked = [got.T[t * slots : (t + 1) * slots].reshape(8, 8, got.shape[0]) for t in range(2)]
    both_steps = jnp.concatenate(picked, axis=1).astype(jnp.bfloat16)
    for dst in range(8):
        contrib[dst % 2, dst // 2] = both_steps[dst]

    def tok_across():
        return remote(contrib.at[flip], tok_in.at[2], tok_send.at[2], tok_recv.at[2], across)

    def tok_along(side):
        return remote(tok_out.at[side], tok_in.at[side], tok_send.at[side], tok_recv.at[side], onward(side))

    def tok_await(side):
        pltpu.make_async_copy(tok_in.at[side], tok_in.at[side], tok_recv.at[side]).wait()

    tok_across().start()

    def plus(a, b):
        return (a.astype(jnp.float32) + b.astype(jnp.float32)).astype(jnp.bfloat16)

    def token_turn(t):
        @pl.when(t == 0)
        def _():
            tok_await(2)
            tokens[...] = plus(contrib[y], tok_in[2])

        for side in range(2):
            place = z if side == 0 else last - z

            @pl.when(place == t)
            def _():
                @pl.when(t > 0)
                def _():
                    tok_await(side)
                    tok_out[side] = plus(tokens[...], tok_in[side])

                @pl.when(t == 0)
                def _():
                    tok_out[side] = tokens[...]

                @pl.when(t < last)
                def _():
                    tok_along(side).start()

    loads[1].wait()

    def head_pair(p, carry):
        cols = pl.ds(pl.multiple_of(p * 384, 128), 384)
        both = jnp.concatenate([queries[0, :, cols].astype(jnp.float32), queries[1, :, cols].astype(jnp.float32)], axis=0)
        for j in range(2):
            h = p * 2 + j
            nope = both[:, 192 * j : 192 * j + 128].astype(jnp.bfloat16)
            rope = both[:, 192 * j + 128 : 192 * j + 192].astype(jnp.bfloat16)
            rows = pl.ds(pl.multiple_of(h * 16, 16), 16)
            q_all[rows, :512] = jnp.dot(nope, uk_v[h], preferred_element_type=jnp.float32).astype(jnp.bfloat16)
            q_all[rows, 512:] = rope
        return carry

    total = row_of.shape[0]
    block_here = jnp.int32(0)
    for b in range(8):
        block_here = block_here + jnp.where(decode_perm[b] == me, b, 0)
    sample = block_here * 8 + lax.broadcasted_iota(jnp.int32, (total, 128), 0) % 8
    prompt = jnp.zeros((total, 128), jnp.int32)
    ends = jnp.int32(0)
    for p in range(prompts):
        ends = ends + counts[p]
        prompt = prompt + jnp.where(sample >= ends, 1, 0)
    rows_vec = jnp.zeros((total, 128), jnp.int32)
    for p in range(prompts):
        rows_vec = jnp.where(prompt == p, prompt_rows[p], rows_vec)
    row_of[...] = rows_vec
    m_ref[...] = jnp.full_like(m_ref, masked_fill)
    l_ref[...] = jnp.zeros_like(l_ref)
    acc[...] = jnp.zeros_like(acc)
    loads[2].wait()

    score_scale = (NOPE_DIM + ROPE_DIM) ** (-0.5)

    def add_new():
        fresh = (
            tok_out[0, z].astype(jnp.float32) + tok_out[1, z].astype(jnp.float32) - tokens[z].astype(jnp.float32)
        )
        rope = fresh[:, 512:]
        swap = lax.broadcasted_iota(jnp.int32, (64, 64), 0) == (lax.broadcasted_iota(jnp.int32, (64, 64), 1) + 32) % 64
        swapped = jnp.dot(
            rope.astype(jnp.bfloat16), jnp.where(swap, 1.0, 0.0).astype(jnp.bfloat16), preferred_element_type=jnp.float32
        )
        new_keys[:, :512] = fresh[:, :512].astype(jnp.bfloat16)
        new_keys[:, 512:] = (rope * rope_cos[...] + swapped * rope_sin[...]).astype(jnp.bfloat16)
        scores = contract_last(q_all[...], new_keys[...]) * score_scale
        row = lax.broadcasted_iota(jnp.int32, (total, 16), 0) % 16
        key = lax.broadcasted_iota(jnp.int32, (total, 16), 1)
        seen = (row % 8 == key % 8) & (key // 8 <= row // 8)
        scores = jnp.where(seen, scores, masked_fill)
        before = m_ref[...]
        top = jnp.maximum(before, jnp.max(scores, axis=1, keepdims=True))
        fade = jnp.exp(before - top)
        probs = jnp.exp(scores - top[:, :16])
        m_ref[...] = top
        l_ref[...] = l_ref[...] * fade + jnp.sum(probs, axis=1, keepdims=True)
        gained = jnp.dot(probs.astype(jnp.bfloat16), new_keys[:, :512], preferred_element_type=jnp.float32)
        acc[...] = acc[...] * jnp.concatenate([fade] * 4, axis=1) + gained

    def attend(src):
        keys = jnp.concatenate([kv[src, r] for r in range(prompts)], axis=1)
        scores = jnp.dot(q_all[...], keys, preferred_element_type=jnp.float32)
        rows = row_of[...]
        chosen = scores[:, :block]
        for r in range(1, prompts):
            chosen = jnp.where(rows == r, scores[:, r * block : (r + 1) * block], chosen)
        chosen = chosen * score_scale
        before = m_ref[...]
        top = jnp.maximum(before, jnp.max(chosen, axis=1, keepdims=True))
        fade = jnp.exp(before - top)
        probs = jnp.exp(chosen - top)
        m_ref[...] = top
        l_ref[...] = l_ref[...] * fade + jnp.sum(probs, axis=1, keepdims=True)
        spread = jnp.concatenate([jnp.where(rows == r, probs, 0.0).astype(jnp.bfloat16) for r in range(prompts)], axis=1)
        gained = contract_last(spread, keys[:512])
        acc[...] = acc[...] * jnp.concatenate([fade] * 4, axis=1) + gained

    def gather_turn(t, carry):
        cache.turn(t)

        @pl.when(t < 2)
        def _():
            pairs = head_count // 4
            lax.fori_loop(t * pairs, t * pairs + pairs, head_pair, 0)

        @pl.when(t <= last)
        def _():
            token_turn(t)

        @pl.when(t == last + 1)
        def _():
            add_new()

        def one(j, c):
            k = 2 * t - 5 + j

            @pl.when((k >= 0) & (k < 8))
            def _():
                src = 2 * layer(k // 2) + jnp.where(k % 2 == 0, y, flip)

                @pl.when(k > 0)
                def _():
                    await_sibling(src)

                attend(src)

            return c

        @pl.when(t >= 2)
        def _():
            lax.fori_loop(0, 2, one, 0)

        return carry

    lax.fori_loop(0, turns, gather_turn, 0)

    att[...] = (acc[...] * jnp.concatenate([1.0 / l_ref[...]] * 4, axis=1)).astype(jnp.bfloat16)
    loads[3].wait()

    per_piece = head_count // 2

    def up_value(step, carry):
        got = []
        for j in range(4):
            h = step * 4 + j
            rows = pl.ds(pl.multiple_of(h * 16, 16), 16)
            got.append(jnp.dot(att[rows, :], uv_v[h], preferred_element_type=jnp.float32))
        spot = (step * 4) % per_piece
        wide = jnp.concatenate(got, axis=1).astype(jnp.bfloat16)
        heads_all[step * 4 // per_piece, me, :, pl.ds(pl.multiple_of(spot * 128, 128), 512)] = wide
        return carry

    shared = Relay(lambda src, q: heads_all.at[q, src], lambda src, q: ho_recv.at[src, q], ho_own, ho_z, ho_y)
    for q in range(2):
        lax.fori_loop(q * per_piece // 4, (q + 1) * per_piece // 4, up_value, 0)
        shared.mine(q, lambda c: c.start())

    def share_turn(t, carry):
        shared.turn(t)
        return carry

    lax.fori_loop(0, turns, share_turn, 0)
    loads[4].wait()

    depth = 512
    rows_out = part.shape[0]
    part[...] = jnp.zeros_like(part)
    per_half = wout_v.shape[0] // 2 // depth

    def project(k, carry):
        cols = pl.ds(pl.multiple_of((k % per_half) * depth, depth), depth)
        left = heads_all[k // per_half, :, :, cols].reshape(rows_out, depth)
        rows = pl.ds(pl.multiple_of(k * depth, depth), depth)
        part[...] += jnp.dot(left, wout_v[rows, :], preferred_element_type=jnp.float32)
        return carry

    lax.fori_loop(0, wout_v.shape[0] // depth, project, 0)

    kept = rows_out // 2
    swap_copy = remote(
        part.at[pl.ds(pl.multiple_of((1 - core) * kept, kept), kept)], other, ex_sem.at[0], ex_sem.at[1], sibling
    )
    swap_copy.start()

    cache.settle()
    shared.settle()
    tok_across().wait_send()

    @pl.when(z < last)
    def _():
        tok_along(0).wait_send()

    @pl.when(z > 0)
    def _():
        tok_along(1).wait_send()

    swap_copy.wait()
    summed = part[pl.ds(pl.multiple_of(core * kept, kept), kept), :] + other[...]
    out[...] = summed.astype(out.dtype)


def rope_tables(first, step_count, slots):
    half_dim = ROPE_DIM // 2
    freqs = np.float32(rope_base) ** (-np.arange(half_dim, dtype=np.float32) / np.float32(half_dim))
    angles = (first + np.arange(step_count)).astype(np.float32)[:, None] * freqs.astype(np.float32)[None, :]
    cosine = np.cos(angles.astype(np.float64)).astype(np.float32)
    sine = np.sin(angles.astype(np.float64)).astype(np.float32)
    return (
        np.repeat(np.concatenate([cosine, cosine], axis=1), slots, axis=0),
        np.repeat(np.concatenate([-sine, sine], axis=1), slots, axis=0),
    )


def fused_shards(store, queries, table, w_uk, w_uv, w_out, counts, prompt_rows, decode_perm, token_ids):
    roll_count = lax.axis_size("roll")
    step_count, slots_dev = queries.shape[:2]
    prompts, block, latent = store.shape
    head_count = w_uk.shape[0]
    rows_q = head_count * step_count * slots_dev
    rows_out = roll_count * step_count * slots_dev
    width = w_out.shape[1]
    cos_rows, sin_rows = rope_tables(block * roll_count, step_count, slots_dev)
    bf16, f32 = jnp.bfloat16, jnp.float32
    smem = pl.BlockSpec(memory_space=pltpu.SMEM)
    vmem = pl.BlockSpec(memory_space=pltpu.VMEM)
    anywhere = pl.BlockSpec(memory_space=pl.ANY)
    dma = pltpu.SemaphoreType.DMA
    summed = pl.pallas_call(
        fused_kernel,
        out_shape=jax.ShapeDtypeStruct((rows_out // 2, width), bf16),
        in_specs=[smem, smem, smem, vmem, vmem, vmem, vmem] + [anywhere] * 5,
        out_specs=vmem,
        scratch_shapes=[
            pltpu.VMEM((roll_count, prompts, latent, block), bf16),
            pltpu.VMEM((latent, table.shape[0]), bf16),
            pltpu.VMEM(w_uk.shape, bf16),
            pltpu.VMEM(w_uv.shape, bf16),
            pltpu.VMEM(w_out.shape, bf16),
            pltpu.VMEM((2, roll_count // 2, 16, latent), bf16),
            pltpu.VMEM((roll_count // 2, 16, latent), bf16),
            pltpu.VMEM((3, roll_count // 2, 16, latent), bf16),
            pltpu.VMEM((2, roll_count // 2, 16, latent), bf16),
            pltpu.VMEM((16, latent), bf16),
            pltpu.VMEM((rows_q, latent), bf16),
            pltpu.VMEM((rows_q, 128), jnp.int32),
            pltpu.VMEM((rows_q, 128), f32),
            pltpu.VMEM((rows_q, 128), f32),
            pltpu.VMEM((rows_q, KV_RANK), f32),
            pltpu.VMEM((rows_q, KV_RANK), bf16),
            pltpu.VMEM((2, roll_count, 16, w_out.shape[0] // 2), bf16),
            pltpu.VMEM((rows_out, width), f32),
            pltpu.VMEM((rows_out // 2, width), f32),
            dma((5,)), dma((8, 4)), dma((4, 2)), dma((2, 7)), dma((2, 7)), dma((2,)), dma((2, 7)), dma((2, 7)),
            dma((3,)), dma((3,)), dma((8, 2)), dma((4, 2)), dma((2, 7)), dma((2, 7)), dma((2,)),
        ],
        compiler_params=pltpu.CompilerParams(
            collective_id=0, has_side_effects=True, vmem_limit_bytes=56 * 1024 * 1024
        ),
        name="fused_attention",
    )(
        counts, prompt_rows, decode_perm, token_ids.T, jnp.asarray(cos_rows), jnp.asarray(sin_rows), queries,
        store.transpose(0, 2, 1), table.T, w_uk, w_uv, w_out,
    )
    by_slot = summed.reshape(-1, step_count, slots_dev, width).transpose(0, 2, 1, 3)
    return by_slot.reshape(-1, step_count, width)


def solution(mesh):
    body = fused_shards if mesh.shape["roll"] == 8 and mesh.shape["head"] == 2 else shards
    in_specs = (
        P("grp", "roll", None),
        P(None, ("grp", "roll"), "head"),
        P("roll", None),
        P("head", None, None),
        P("head", None, None),
        P("head", "roll"),
        P("grp"),
        P("grp"),
        P("grp"),
        P("grp", None),
    )
    out_specs = P(("grp", "head"), None, "roll")
    return jax.shard_map(body, mesh=mesh, in_specs=in_specs, out_specs=out_specs, check_vma=False)
```

```python
import functools

import jax
import jax.numpy as jnp
import numpy as np
from jax import lax
from jax.experimental import pallas as pl
from jax.experimental.pallas import tpu as pltpu
from jax.sharding import PartitionSpec as P

KV_RANK = 512
ROPE_DIM = 64
NOPE_DIM = 128


masked_fill = -1e30
rope_base = 10000.0


def pick_values(values, positions):
    matches = positions[..., None] == jnp.arange(values.shape[0], dtype=jnp.int32)
    return jnp.sum(jnp.where(matches, values, 0), axis=-1)


def rotate_rope(latent_rows, positions):
    half_dim = ROPE_DIM // 2
    freqs = rope_base ** (-jnp.arange(half_dim, dtype=jnp.float32) / half_dim)
    angles = positions[:, None] * freqs[None, :]
    cosine = jnp.cos(angles)
    sine = jnp.sin(angles)
    front = latent_rows[..., KV_RANK : KV_RANK + half_dim]
    behind = latent_rows[..., KV_RANK + half_dim :]
    return jnp.concatenate(
        [
            latent_rows[..., :KV_RANK],
            front * cosine - behind * sine,
            front * sine + behind * cosine,
        ],
        axis=-1,
    )


def shards(store, queries, table, w_uk, w_uv, w_out, counts, prompt_rows, decode_perm, token_ids):
    roll_count = lax.axis_size("roll")
    roll_index = lax.axis_index("roll")
    step_count = queries.shape[0]
    slots_dev = queries.shape[1]
    latent_width = store.shape[2]
    cache_len = store.shape[1] * roll_count
    bound_ends = jnp.cumsum(counts)
    sample_ids = jnp.arange(roll_count * slots_dev, dtype=jnp.int32)
    prompt_of = jnp.sum((bound_ends[None, :] <= sample_ids[:, None]).astype(jnp.int32), axis=1)
    devices = jnp.arange(roll_count, dtype=jnp.int32)
    block_of = jnp.sum(
        jnp.where(decode_perm[None, :] == devices[:, None], devices[None, :], 0), axis=1
    )
    slot_offsets = jnp.arange(slots_dev, dtype=jnp.int32)
    slot_prompt = pick_values(prompt_of, block_of[:, None] * slots_dev + slot_offsets[None, :])
    send_rows = pick_values(prompt_rows, slot_prompt).reshape(-1)
    outgoing = jnp.take(store, send_rows, axis=0).reshape(
        roll_count, slots_dev, store.shape[1], latent_width
    )
    incoming = lax.all_to_all(outgoing, "roll", split_axis=0, concat_axis=2, tiled=True)
    cache_rows = incoming.reshape(slots_dev, cache_len, latent_width)
    flat_ids = token_ids.reshape(-1)
    vocab_dev = table.shape[0]
    vocab_base = roll_index * vocab_dev
    one_hot = (
        flat_ids[:, None] - vocab_base == jnp.arange(vocab_dev, dtype=jnp.int32)[None, :]
    ).astype(jnp.bfloat16)
    looked = lax.psum_scatter(
        jnp.dot(one_hot, table, preferred_element_type=jnp.float32),
        "roll",
        scatter_dimension=0,
        tiled=True,
    )
    looked = (
        looked.astype(jnp.bfloat16).astype(jnp.float32).reshape(slots_dev, step_count, latent_width)
    )
    positions = (cache_len + jnp.arange(step_count)).astype(jnp.float32)
    new_latents = rotate_rope(looked, positions).astype(jnp.bfloat16)
    head_count = w_uk.shape[0]
    query_parts = queries.reshape(step_count, slots_dev, head_count, -1)
    q_latent = jnp.einsum(
        "tshd,hdc->tshc", query_parts[..., :NOPE_DIM], w_uk, preferred_element_type=jnp.float32
    ).astype(jnp.bfloat16)
    q_full = jnp.concatenate([q_latent, query_parts[..., NOPE_DIM:]], axis=-1)
    score_scale = (NOPE_DIM + ROPE_DIM) ** (-0.5)
    cache_scores = (
        jnp.einsum("tshc,sjc->tshj", q_full, cache_rows, preferred_element_type=jnp.float32)
        * score_scale
    )
    new_scores = (
        jnp.einsum("tshc,suc->tshu", q_full, new_latents, preferred_element_type=jnp.float32)
        * score_scale
    )
    allowed = jnp.arange(step_count)[None, :] <= jnp.arange(step_count)[:, None]
    new_scores = jnp.where(allowed[:, None, None, :], new_scores, masked_fill)
    row_max = jnp.maximum(jnp.max(cache_scores, axis=-1), jnp.max(new_scores, axis=-1))[..., None]
    cache_exp = jnp.exp(cache_scores - row_max)
    new_exp = jnp.exp(new_scores - row_max)
    denom = jnp.sum(cache_exp, axis=-1, keepdims=True) + jnp.sum(new_exp, axis=-1, keepdims=True)
    cache_probs = (cache_exp / denom).astype(jnp.bfloat16)
    new_probs = (new_exp / denom).astype(jnp.bfloat16)
    attended = jnp.einsum(
        "tshj,sjc->tshc", cache_probs, cache_rows[..., :KV_RANK], preferred_element_type=jnp.float32
    )
    attended = attended + jnp.einsum(
        "tshu,suc->tshc", new_probs, new_latents[..., :KV_RANK], preferred_element_type=jnp.float32
    )
    attended = attended.astype(jnp.bfloat16)
    head_out = jnp.einsum(
        "tshc,hcv->tshv", attended, w_uv, preferred_element_type=jnp.float32
    ).astype(jnp.bfloat16)
    slot_major = head_out.transpose(1, 0, 2, 3).reshape(slots_dev * step_count, -1)
    partial_out = jnp.dot(
        lax.all_gather(slot_major, "roll", axis=0, tiled=True),
        w_out,
        preferred_element_type=jnp.float32,
    )
    summed = lax.psum_scatter(partial_out, "head", scatter_dimension=0, tiled=True)
    return summed.astype(jnp.bfloat16).reshape(-1, step_count, w_out.shape[1])


def contract_last(a, b):
    return lax.dot_general(a, b, (((1,), (1,)), ((), ())), preferred_element_type=jnp.float32)


def fused_kernel(
    counts, prompt_rows, decode_perm, token_ids, rope_cos, rope_sin, queries, store, table, w_uk, w_uv, w_out,
    out,
    kv, table_v, uk_v, uv_v, wout_v, contrib, tokens, tok_in, tok_out, new_keys, q_all, row_of, m_ref, l_ref, acc, att, heads_all, part, other,
    load_sem, kv_recv, kv_own, kv_z, kv_y, sib_own, sib_z, sib_y, tok_recv, tok_send,
    ho_recv, ho_own, ho_z, ho_y, ex_sem,
):
    me = lax.axis_index("roll")
    core = lax.axis_index("head")
    z, y = me // 2, me % 2
    flip = 1 - y
    prompts = store.shape[0]
    half = prompts // 2
    block = store.shape[2]
    head_count = uk_v.shape[0]
    last = 3

    def to(roll):
        return {"roll": roll}

    sibling = {"head": 1 - core}
    def remote(src, dst, send, recv, device):
        return pltpu.make_async_remote_copy(
            src_ref=src, dst_ref=dst, send_sem=send, recv_sem=recv, device_id=device,
            device_id_type=pl.DeviceIdType.MESH,
        )

    loads = [
        pltpu.make_async_copy(table, table_v, load_sem.at[0]),
        pltpu.make_async_copy(w_uk, uk_v, load_sem.at[1]),
        pltpu.make_async_copy(store, kv.at[me], load_sem.at[2]),
        pltpu.make_async_copy(w_uv, uv_v, load_sem.at[3]),
        pltpu.make_async_copy(w_out, wout_v, load_sem.at[4]),
    ]
    for load in loads:
        load.start()

    barrier = pltpu.get_barrier_semaphore()
    def greet(device):
        pl.semaphore_signal(barrier, inc=1, device_id=device, device_id_type=pl.DeviceIdType.MESH)

    greet(to(z * 2 + flip))
    greet(sibling)

    @pl.when(z < last)
    def _():
        greet(to(me + 2))

    @pl.when(z > 0)
    def _():
        greet(to(me - 2))

    pl.semaphore_wait(barrier, 2 + jnp.where(z < last, 1, 0) + jnp.where(z > 0, 1, 0))

    near = jnp.minimum(z, last - z)

    def layer(i):
        up = jnp.where(i == 0, near, jnp.where(i > near, i, i - 1))
        return jnp.where(z <= 1, up, last - up)

    def from_side(side, t):
        layers = z if side == 0 else last - z
        extra = t == 2 * layers
        away = jnp.minimum(t // 2, layers - 1) + 1
        origin = jnp.where(extra, flip, y) + 2 * (z - away if side == 0 else z + away)
        crossed = 2 * (z - away if side == 0 else z + away) + flip
        comes = (layers > 0) & (t <= 2 * layers)
        goes_on = comes & (z < last if side == 0 else z > 0)
        return origin, jnp.where(extra, 1, t % 2), comes, goes_on, t < 2 * layers - 1, crossed

    def onward(side):
        return to(me + 2 if side == 0 else me - 2)

    across = to(z * 2 + flip)

    class Relay:
        def __init__(self, piece, recv, own, along, over, swap=None):
            self.piece, self.recv, self.own, self.along, self.over, self.swap = piece, recv, own, along, over, swap

        def send(self, src, q, sem, device):
            return remote(self.piece(src, q), self.piece(src, q), sem, self.recv(src, q), device)

        def arrive(self, src, q):
            ref = self.piece(src, q)
            pltpu.make_async_copy(ref, ref, self.recv(src, q)).wait()

        def mine(self, q, act):
            act(self.send(me, q, self.own.at[2, q], across))
            for side in range(2):

                @pl.when(z < last if side == 0 else z > 0)
                def _():
                    act(self.send(me, q, self.own.at[side, q], onward(side)))

        def end_extra(self, act):
            for side in range(2):

                @pl.when(z == 0 if side == 0 else z == last)
                def _():
                    act(self.send(z * 2 + flip, 1, self.own.at[3, side], onward(side)))

        def along_turn(self, t):
            for side in range(2):
                src, q, comes, goes_on, crosses, _ = from_side(side, t)

                @pl.when(comes)
                def _():
                    self.arrive(src, q)

                    @pl.when(goes_on)
                    def _():
                        self.send(src, q, self.along.at[side, t], onward(side)).start()

                    @pl.when(crosses)
                    def _():
                        self.send(src, q, self.over.at[side, t], across).start()

                    if self.swap:
                        self.send(src, q, self.swap[1].at[side, t], sibling).start()

        def own_crossed(self, t):
            self.arrive(z * 2 + flip, t)
            if self.swap:
                self.send(z * 2 + flip, t, self.swap[0].at[t], sibling).start()

        def crossed_turn(self, t):
            for side in range(2):
                _, q, _, _, crosses, src = from_side(side, t)

                @pl.when(crosses)
                def _():
                    self.arrive(src, q)
                    if self.swap:
                        self.send(src, q, self.swap[2].at[side, t], sibling).start()

        def turn(self, t):
            self.along_turn(t)

            @pl.when(t < 2)
            def _():
                self.own_crossed(t)

            @pl.when(t == 1)
            def _():
                self.end_extra(lambda c: c.start())

            @pl.when(t >= 2)
            def _():
                self.crossed_turn(t - 2)

        def settle(self):
            def leave(c):
                c.wait_send()

            for q in range(2):
                self.mine(q, leave)
                if self.swap:
                    leave(self.send(z * 2 + flip, q, self.swap[0].at[q], sibling))
            self.end_extra(leave)

            def one(t, carry):
                for side in range(2):
                    src, q, comes, goes_on, crosses, other_src = from_side(side, t)

                    @pl.when(goes_on)
                    def _():
                        leave(self.send(src, q, self.along.at[side, t], onward(side)))

                    @pl.when(crosses)
                    def _():
                        leave(self.send(src, q, self.over.at[side, t], across))

                    if self.swap:

                        @pl.when(comes)
                        def _():
                            leave(self.send(src, q, self.swap[1].at[side, t], sibling))

                        @pl.when(crosses)
                        def _():
                            leave(self.send(other_src, q, self.swap[2].at[side, t], sibling))

                return carry

            lax.fori_loop(0, turns, one, 0)

    turns = 7
    cache = Relay(
        lambda src, q: kv.at[src, half * core + q],
        lambda src, q: kv_recv.at[src, half * core + q],
        kv_own, kv_z, kv_y, (sib_own, sib_z, sib_y),
    )

    def await_sibling(src):
        for q in range(half):
            r = half * (1 - core) + q
            pltpu.make_async_copy(kv.at[src, r], kv.at[src, r], kv_recv.at[src, r]).wait()

    def send_own_cache(q, act):
        own = store.at[half * core + q]
        here = kv.at[me, half * core + q]
        sem = kv_recv.at[me, half * core + q]
        act(remote(own, here, kv_own.at[2, q], sem, across))
        for side in range(2):

            @pl.when(z < last if side == 0 else z > 0)
            def _():
                act(remote(own, here, kv_own.at[side, q], sem, onward(side)))

    cache.mine = send_own_cache
    for q in range(2):
        cache.mine(q, lambda c: c.start())

    loads[0].wait()
    rows_here = table_v.shape[1]
    slots = token_ids.shape[1]
    ids = jnp.concatenate([token_ids[0:1, :], token_ids[1:2, :]], axis=1)
    spots = lax.broadcasted_iota(jnp.int32, (rows_here, 2 * slots), 0) + me * rows_here
    hot = jnp.where(ids == spots, 1.0, 0.0).astype(jnp.bfloat16)
    got = jnp.dot(table_v[...], hot, preferred_element_type=jnp.float32)
    picked = [got.T[t * slots : (t + 1) * slots].reshape(8, 8, got.shape[0]) for t in range(2)]
    both_steps = jnp.concatenate(picked, axis=1).astype(jnp.bfloat16)
    for dst in range(8):
        contrib[dst % 2, dst // 2] = both_steps[dst]

    def tok_across():
        return remote(contrib.at[flip], tok_in.at[2], tok_send.at[2], tok_recv.at[2], across)

    def tok_along(side):
        return remote(tok_out.at[side], tok_in.at[side], tok_send.at[side], tok_recv.at[side], onward(side))

    def tok_await(side):
        pltpu.make_async_copy(tok_in.at[side], tok_in.at[side], tok_recv.at[side]).wait()

    tok_across().start()

    def plus(a, b):
        return (a.astype(jnp.float32) + b.astype(jnp.float32)).astype(jnp.bfloat16)

    def token_turn(t):
        @pl.when(t == 0)
        def _():
            tok_await(2)
            tokens[...] = plus(contrib[y], tok_in[2])

        for side in range(2):
            place = z if side == 0 else last - z

            @pl.when(place == t)
            def _():
                @pl.when(t > 0)
                def _():
                    tok_await(side)
                    tok_out[side] = plus(tokens[...], tok_in[side])

                @pl.when(t == 0)
                def _():
                    tok_out[side] = tokens[...]

                @pl.when(t < last)
                def _():
                    tok_along(side).start()

    loads[1].wait()

    def head_pair(p, carry):
        cols = pl.ds(pl.multiple_of(p * 384, 128), 384)
        both = jnp.concatenate([queries[0, :, cols].astype(jnp.float32), queries[1, :, cols].astype(jnp.float32)], axis=0)
        for j in range(2):
            h = p * 2 + j
            nope = both[:, 192 * j : 192 * j + 128].astype(jnp.bfloat16)
            rope = both[:, 192 * j + 128 : 192 * j + 192].astype(jnp.bfloat16)
            rows = pl.ds(pl.multiple_of(h * 16, 16), 16)
            q_all[rows, :512] = jnp.dot(nope, uk_v[h], preferred_element_type=jnp.float32).astype(jnp.bfloat16)
            q_all[rows, 512:] = rope
        return carry

    total = row_of.shape[0]
    block_here = jnp.int32(0)
    for b in range(8):
        block_here = block_here + jnp.where(decode_perm[b] == me, b, 0)
    sample = block_here * 8 + lax.broadcasted_iota(jnp.int32, (total, 128), 0) % 8
    prompt = jnp.zeros((total, 128), jnp.int32)
    ends = jnp.int32(0)
    for p in range(prompts):
        ends = ends + counts[p]
        prompt = prompt + jnp.where(sample >= ends, 1, 0)
    rows_vec = jnp.zeros((total, 128), jnp.int32)
    for p in range(prompts):
        rows_vec = jnp.where(prompt == p, prompt_rows[p], rows_vec)
    row_of[...] = rows_vec
    m_ref[...] = jnp.full_like(m_ref, masked_fill)
    l_ref[...] = jnp.zeros_like(l_ref)
    acc[...] = jnp.zeros_like(acc)
    loads[2].wait()

    score_scale = (NOPE_DIM + ROPE_DIM) ** (-0.5)

    def add_new():
        fresh = (
            tok_out[0, z].astype(jnp.float32) + tok_out[1, z].astype(jnp.float32) - tokens[z].astype(jnp.float32)
        )
        rope = fresh[:, 512:]
        swap = lax.broadcasted_iota(jnp.int32, (64, 64), 0) == (lax.broadcasted_iota(jnp.int32, (64, 64), 1) + 32) % 64
        swapped = jnp.dot(
            rope.astype(jnp.bfloat16), jnp.where(swap, 1.0, 0.0).astype(jnp.bfloat16), preferred_element_type=jnp.float32
        )
        new_keys[:, :512] = fresh[:, :512].astype(jnp.bfloat16)
        new_keys[:, 512:] = (rope * rope_cos[...] + swapped * rope_sin[...]).astype(jnp.bfloat16)
        scores = contract_last(q_all[...], new_keys[...]) * score_scale
        row = lax.broadcasted_iota(jnp.int32, (total, 16), 0) % 16
        key = lax.broadcasted_iota(jnp.int32, (total, 16), 1)
        seen = (row % 8 == key % 8) & (key // 8 <= row // 8)
        scores = jnp.where(seen, scores, masked_fill)
        before = m_ref[...]
        top = jnp.maximum(before, jnp.max(scores, axis=1, keepdims=True))
        fade = jnp.exp(before - top)
        probs = jnp.exp(scores - top[:, :16])
        m_ref[...] = top
        l_ref[...] = l_ref[...] * fade + jnp.sum(probs, axis=1, keepdims=True)
        gained = jnp.dot(probs.astype(jnp.bfloat16), new_keys[:, :512], preferred_element_type=jnp.float32)
        acc[...] = acc[...] * jnp.concatenate([fade] * 4, axis=1) + gained

    def attend(src):
        keys = jnp.concatenate([kv[src, r] for r in range(prompts)], axis=1)
        scores = jnp.dot(q_all[...], keys, preferred_element_type=jnp.float32)
        rows = row_of[...]
        chosen = scores[:, :block]
        for r in range(1, prompts):
            chosen = jnp.where(rows == r, scores[:, r * block : (r + 1) * block], chosen)
        chosen = chosen * score_scale
        before = m_ref[...]
        top = jnp.maximum(before, jnp.max(chosen, axis=1, keepdims=True))
        fade = jnp.exp(before - top)
        probs = jnp.exp(chosen - top)
        m_ref[...] = top
        l_ref[...] = l_ref[...] * fade + jnp.sum(probs, axis=1, keepdims=True)
        spread = jnp.concatenate([jnp.where(rows == r, probs, 0.0).astype(jnp.bfloat16) for r in range(prompts)], axis=1)
        gained = contract_last(spread, keys[:512])
        acc[...] = acc[...] * jnp.concatenate([fade] * 4, axis=1) + gained

    def gather_turn(t, carry):
        @pl.when(t == turns - 1)
        def _():
            add_new()

        cache.turn(t)

        @pl.when(t < 2)
        def _():
            pairs = head_count // 4
            lax.fori_loop(t * pairs, t * pairs + pairs, head_pair, 0)

        def one(j, c):
            k = 2 * t - 5 + j

            @pl.when((k >= 0) & (k < 8))
            def _():
                src = 2 * layer(k // 2) + jnp.where(k % 2 == 0, y, flip)

                @pl.when(k > 0)
                def _():
                    await_sibling(src)

                attend(src)

            return c

        @pl.when(t >= 2)
        def _():
            lax.fori_loop(0, 2, one, 0)

        @pl.when((t == 1) | ((t >= 3) & (t <= 5)))
        def _():
            token_turn(jnp.where(t == 1, 0, t - 2))

        return carry

    lax.fori_loop(0, turns, gather_turn, 0)

    att[...] = (acc[...] * jnp.concatenate([1.0 / l_ref[...]] * 4, axis=1)).astype(jnp.bfloat16)
    loads[3].wait()

    per_piece = head_count // 2

    def up_value(step, carry):
        got = []
        for j in range(4):
            h = step * 4 + j
            rows = pl.ds(pl.multiple_of(h * 16, 16), 16)
            got.append(jnp.dot(att[rows, :], uv_v[h], preferred_element_type=jnp.float32))
        spot = (step * 4) % per_piece
        wide = jnp.concatenate(got, axis=1).astype(jnp.bfloat16)
        heads_all[step * 4 // per_piece, me, :, pl.ds(pl.multiple_of(spot * 128, 128), 512)] = wide
        return carry

    shared = Relay(lambda src, q: heads_all.at[q, src], lambda src, q: ho_recv.at[src, q], ho_own, ho_z, ho_y)
    for q in range(2):
        lax.fori_loop(q * per_piece // 4, (q + 1) * per_piece // 4, up_value, 0)
        shared.mine(q, lambda c: c.start())

    def share_turn(t, carry):
        shared.turn(t)
        return carry

    lax.fori_loop(0, turns, share_turn, 0)
    loads[4].wait()

    depth = 512
    rows_out = part.shape[0]
    part[...] = jnp.zeros_like(part)
    per_half = wout_v.shape[0] // 2 // depth

    def project(k, carry):
        cols = pl.ds(pl.multiple_of((k % per_half) * depth, depth), depth)
        left = heads_all[k // per_half, :, :, cols].reshape(rows_out, depth)
        rows = pl.ds(pl.multiple_of(k * depth, depth), depth)
        part[...] += jnp.dot(left, wout_v[rows, :], preferred_element_type=jnp.float32)
        return carry

    lax.fori_loop(0, wout_v.shape[0] // depth, project, 0)

    kept = rows_out // 2
    swap_copy = remote(
        part.at[pl.ds(pl.multiple_of((1 - core) * kept, kept), kept)], other, ex_sem.at[0], ex_sem.at[1], sibling
    )
    swap_copy.start()

    cache.settle()
    shared.settle()
    tok_across().wait_send()

    @pl.when(z < last)
    def _():
        tok_along(0).wait_send()

    @pl.when(z > 0)
    def _():
        tok_along(1).wait_send()

    swap_copy.wait()
    summed = part[pl.ds(pl.multiple_of(core * kept, kept), kept), :] + other[...]
    out[...] = summed.astype(out.dtype)


def rope_tables(first, step_count, slots):
    half_dim = ROPE_DIM // 2
    freqs = np.float32(rope_base) ** (-np.arange(half_dim, dtype=np.float32) / np.float32(half_dim))
    angles = (first + np.arange(step_count)).astype(np.float32)[:, None] * freqs.astype(np.float32)[None, :]
    cosine = np.cos(angles.astype(np.float64)).astype(np.float32)
    sine = np.sin(angles.astype(np.float64)).astype(np.float32)
    return (
        np.repeat(np.concatenate([cosine, cosine], axis=1), slots, axis=0),
        np.repeat(np.concatenate([-sine, sine], axis=1), slots, axis=0),
    )


def fused_shards(store, queries, table, w_uk, w_uv, w_out, counts, prompt_rows, decode_perm, token_ids):
    roll_count = lax.axis_size("roll")
    step_count, slots_dev = queries.shape[:2]
    prompts, block, latent = store.shape
    head_count = w_uk.shape[0]
    rows_q = head_count * step_count * slots_dev
    rows_out = roll_count * step_count * slots_dev
    width = w_out.shape[1]
    cos_rows, sin_rows = rope_tables(block * roll_count, step_count, slots_dev)
    bf16, f32 = jnp.bfloat16, jnp.float32
    smem = pl.BlockSpec(memory_space=pltpu.SMEM)
    vmem = pl.BlockSpec(memory_space=pltpu.VMEM)
    anywhere = pl.BlockSpec(memory_space=pl.ANY)
    dma = pltpu.SemaphoreType.DMA
    summed = pl.pallas_call(
        fused_kernel,
        out_shape=jax.ShapeDtypeStruct((rows_out // 2, width), bf16),
        in_specs=[smem, smem, smem, vmem, vmem, vmem, vmem] + [anywhere] * 5,
        out_specs=vmem,
        scratch_shapes=[
            pltpu.VMEM((roll_count, prompts, latent, block), bf16),
            pltpu.VMEM((latent, table.shape[0]), bf16),
            pltpu.VMEM(w_uk.shape, bf16),
            pltpu.VMEM(w_uv.shape, bf16),
            pltpu.VMEM(w_out.shape, bf16),
            pltpu.VMEM((2, roll_count // 2, 16, latent), bf16),
            pltpu.VMEM((roll_count // 2, 16, latent), bf16),
            pltpu.VMEM((3, roll_count // 2, 16, latent), bf16),
            pltpu.VMEM((2, roll_count // 2, 16, latent), bf16),
            pltpu.VMEM((16, latent), bf16),
            pltpu.VMEM((rows_q, latent), bf16),
            pltpu.VMEM((rows_q, 128), jnp.int32),
            pltpu.VMEM((rows_q, 128), f32),
            pltpu.VMEM((rows_q, 128), f32),
            pltpu.VMEM((rows_q, KV_RANK), f32),
            pltpu.VMEM((rows_q, KV_RANK), bf16),
            pltpu.VMEM((2, roll_count, 16, w_out.shape[0] // 2), bf16),
            pltpu.VMEM((rows_out, width), f32),
            pltpu.VMEM((rows_out // 2, width), f32),
            dma((5,)), dma((8, 4)), dma((4, 2)), dma((2, 7)), dma((2, 7)), dma((2,)), dma((2, 7)), dma((2, 7)),
            dma((3,)), dma((3,)), dma((8, 2)), dma((4, 2)), dma((2, 7)), dma((2, 7)), dma((2,)),
        ],
        compiler_params=pltpu.CompilerParams(
            collective_id=0, has_side_effects=True, vmem_limit_bytes=56 * 1024 * 1024
        ),
        name="fused_attention",
    )(
        counts, prompt_rows, decode_perm, token_ids.T, jnp.asarray(cos_rows), jnp.asarray(sin_rows), queries,
        store.transpose(0, 2, 1), table.T, w_uk, w_uv, w_out,
    )
    by_slot = summed.reshape(-1, step_count, slots_dev, width).transpose(0, 2, 1, 3)
    return by_slot.reshape(-1, step_count, width)


def solution(mesh):
    body = fused_shards if mesh.shape["roll"] == 8 and mesh.shape["head"] == 2 else shards
    in_specs = (
        P("grp", "roll", None),
        P(None, ("grp", "roll"), "head"),
        P("roll", None),
        P("head", None, None),
        P("head", None, None),
        P("head", "roll"),
        P("grp"),
        P("grp"),
        P("grp"),
        P("grp", None),
    )
    out_specs = P(("grp", "head"), None, "roll")
    return jax.shard_map(body, mesh=mesh, in_specs=in_specs, out_specs=out_specs, check_vma=False)
```
